1024 devices in a mesh: node: 32 (over z), local: 32 (over x, y, core).
Axes of the slice: x: 4, y: 4, z: 32, core: 2. Of those that a mesh axis runs over, the one named last changes fastest.
Arguments:
- out_grad: bfloat16 [4096, 7168], P('node', 'local'), may hold values from -3 to 3
- node_pick: int32 [4096, 4], P('node'), may hold values from 0 to 31, all different within a row; in each aligned block of 128 rows (0 to 127, 128 to 255, ...) at most 20 rows name the same one
- expert_pick: int32 [4096, 4, 1], P('node'), may hold values from 0 to 1
- pick_weight: bfloat16 [4096, 4, 1], P('node'), may hold values from 0.049804688 to 1
- gate_weight: bfloat16 [32, 2, 7168, 1024], P('node', None, 'local'), may hold values from -0.0625 to 0.0625
- up_weight: bfloat16 [32, 2, 7168, 1024], P('node', None, 'local'), may hold values from -0.0625 to 0.0625
- down_weight: bfloat16 [32, 2, 1024, 7168], P('node', None, None, 'local'), may hold values from -0.1875 to 0.1875
- saved_gate: bfloat16 [32, 640, 1, 1024], P('node', 'local'), may hold values from -5 to 5
- saved_up: bfloat16 [32, 640, 1, 1024], P('node', 'local'), may hold values from -1.1953125 to 1.1953125
Outputs:
- input_grad: bfloat16 [4096, 7168], P('node', 'local')
- router_grad: bfloat16 [4096, 4, 1], P('node')
The draws below stay inside these ranges and needn't reach their ends.
Inputs may be any that keep to these rules, and one draw needn't show every extreme that they name: `node_pick`: each token names 4 different node groups; among the tokens of one node group no node group is named by more than 20 tokens, and one is named by exactly 20. `expert_pick`: the 1 expert of each token and node group are different.
All inputs are finite; a program needn't handle non-finite values.
Results may differ from the reference program's by a relative error of at most 0.0057.
Values may be sent and summed in bfloat16 or wider, within the bound.
No kernel may reach another device: no remote copies, remote signals or barrier semaphores. Data moves between devices by JAX's collectives and lax.ppermute only.
A program may use at most 64 MiB of HBM per device.

```python
import math
import jax
import jax.numpy as jnp
import numpy as np
from jax import lax

D = 7168
FF = 1024
E_NODE = 2
GROUPS = 4
PICKS = 1
TOK_NODE = 128
NODES = 32
CAP_N = 20
SLOTS = 640
TOKENS = 4096


def shard_levels(stream_key, extent, shards, low, largest):
    gain, own = 1.0, jax.random.fold_in(stream_key, 6)
    for axis_at, blocks in shards:
        heights = jnp.exp(jax.random.uniform(jax.random.fold_in(own, axis_at), (blocks,), jnp.float32, low / len(shards), largest / len(shards)))
        gain = gain * jnp.repeat(heights, extent[axis_at] // blocks).reshape([-1 if axis == axis_at else 1 for axis in range(len(extent))])
    return gain


def different_ones(rng, rows, amount, top, lift):
    ranking = jax.random.permutation(jax.random.fold_in(rng, 1), amount)
    boost = ranking
    for power in range(3):
        boost = boost * boost // amount
    boost = boost * lift // amount
    chance = jax.random.randint(jax.random.fold_in(rng, 2), (rows, amount), 0, 4096) + boost
    sure = jax.random.permutation(jax.random.fold_in(rng, 3), rows)[jnp.arange(amount) % rows]
    chance = jnp.where(jnp.arange(rows)[:, None] == sure[None, :], 1 << 14, chance)
    priority = chance * amount + jnp.arange(amount)
    return lax.top_k(priority.astype(jnp.int32), top)[1].astype(jnp.int32)


def routed_block(key, own, number, rows, number_of, top, bound, lean):
    order = jax.random.permutation(key, number_of)
    packed, common = portions_of(number_of, rows * top, bound, lean, True), portions_of(number_of, rows * top, bound, lean, False)
    places = jnp.arange(number_of)

    def named(tallies, rotation):
        used = int((tallies > 0).sum())
        fixed = max(1, used // 4)
        moved = fixed + (places - fixed + rotation * (used - fixed)) % max(1, number_of - fixed)
        return jnp.zeros((number_of,), jnp.int32).at[order[jnp.where(places < fixed, places, moved)]].set(jnp.asarray(tallies, jnp.int32))

    tallies = jnp.where(number % 4 == 0, named(packed, number // 4), named(common, number - number // 4 - 1))
    mixed = jax.random.permutation(jax.random.fold_in(own, 3), number_of)
    source_of, receiver = mixed[0:number_of // 2 * 2:2], mixed[1:number_of // 2 * 2:2]
    room = jnp.minimum(tallies[source_of] - 1, bound - tallies[receiver]) // 2
    room = jnp.where((source_of == order[0]) | (receiver == order[0]) | (tallies[receiver] == 0), 0, jnp.maximum(room, 0))
    moved = jax.random.randint(jax.random.fold_in(own, 4), (number_of // 2,), 0, 1 << 20) % (room + 1)
    tallies = tallies.at[source_of].add(-moved).at[receiver].add(moved)
    items = jnp.searchsorted(jnp.cumsum(tallies), jnp.arange(rows * top), side="right").astype(jnp.int32)
    table = items.reshape(top, rows).T
    table = table[jax.random.permutation(jax.random.fold_in(own, 1), rows)]
    rotation = jax.random.randint(jax.random.fold_in(own, 2), (rows, 1), 0, top)
    return jnp.take_along_axis(table, (jnp.arange(top)[None, :] + rotation) % top, axis=1)


def portions_of(count, total, bound, lean, full):
    weights = [(1 << 20) // math.isqrt(rank ** lean) + 1 for rank in range(1, count + 1)]
    largest = bound if full else min(bound, max(-(-total // count), total * weights[0] // sum(weights)))
    least = 1 if total - largest >= count - 1 else 0
    given, surplus = [largest] + [least] * (count - 1), total - largest - least * (count - 1)
    while surplus > 0:
        movable = [i for i in range(1, count) if given[i] < largest] or [i for i in range(1, count) if given[i] < bound]
        mass, remaining = sum([weights[i] for i in movable]), surplus
        for i in movable:
            extra = min(bound - given[i], max(1, remaining * weights[i] // mass), surplus)
            given[i] = given[i] + extra
            surplus = surplus - extra
    return np.array(given)


def gaussian(key, shape, scale, reach, pieces=(), kind=jnp.bfloat16):
    factor_of = shard_levels(key, shape, pieces, -0.22, 0.18) if pieces else 1.0
    entries = jax.random.normal(key, shape, jnp.float32) * scale * factor_of
    return jnp.minimum(jnp.maximum(entries, -reach), reach).astype(kind)


def setup_inputs(seed: int = 0) -> dict:
    key_list = jax.random.split(jax.random.key(seed), 10)
    out_grad = gaussian(key_list[0], (TOKENS, D), 0.5, 3.0, ((0, 32), (1, 32)))
    node_pick_keys = jax.random.split(jax.random.fold_in(key_list[1], 1), TOKENS // TOK_NODE)
    node_pick_turns = jax.random.permutation(jax.random.fold_in(key_list[1], 3), TOKENS // TOK_NODE)
    node_pick = jax.vmap(lambda own, number: routed_block(jax.random.fold_in(key_list[1], 2), own, number, TOK_NODE, NODES, GROUPS, CAP_N, 2))(node_pick_keys, node_pick_turns).reshape((TOKENS, GROUPS))
    expert_pick = different_ones(key_list[2], TOKENS * GROUPS, E_NODE, PICKS, 8192).reshape((TOKENS, GROUPS, PICKS))
    pick_weight = jnp.clip(jnp.exp(math.log(1.0) - 2.9996462 * jax.random.uniform(key_list[3], (TOKENS, GROUPS, PICKS), jnp.float32) ** shard_levels(key_list[3], (TOKENS, GROUPS, PICKS), ((0, 32),), -0.2, 0.2)), 0.049804688, 1.0).astype(jnp.bfloat16)
    gate_weight = gaussian(key_list[4], (NODES, E_NODE, D, FF), D ** -0.5, 0.0625, ((0, 32), (2, 32)))
    up_weight = gaussian(key_list[5], (NODES, E_NODE, D, FF), D ** -0.5, 0.0625, ((0, 32), (2, 32)))
    down_weight = gaussian(key_list[6], (NODES, E_NODE, FF, D), FF ** -0.5, 0.1875, ((0, 32), (3, 32)))
    saved_gate = gaussian(key_list[7], (NODES, SLOTS, PICKS, FF), 1.0, 5.0, ((0, 32), (1, 32)))
    saved_up = gaussian(key_list[8], (NODES, SLOTS, PICKS, FF), 0.2, 1.1953125, ((0, 32), (1, 32)))
    return dict(out_grad=out_grad, node_pick=node_pick, expert_pick=expert_pick, pick_weight=pick_weight, gate_weight=gate_weight, up_weight=up_weight, down_weight=down_weight, saved_gate=saved_gate, saved_up=saved_up)


def arrival(node_pick):
    target = node_pick.reshape(NODES, TOK_NODE * GROUPS).astype(jnp.int32)
    matches = (target[:, :, None] == jnp.arange(NODES, dtype=jnp.int32)[None, None, :]).astype(jnp.int32)
    before = jnp.cumsum(matches, axis=1) - matches
    position = jnp.sum(before * matches, axis=2).astype(jnp.int32)
    source = jnp.arange(NODES, dtype=jnp.int32)[:, None]
    return (target * SLOTS + source * CAP_N + position).astype(jnp.int32).reshape(TOKENS, GROUPS)


def node_backward(operands):
    arrived, picked, weight_row, gate_node, up_node, down_node, gate_stored, up_stored = operands
    raw_all = jnp.einsum("sd,efd->sef", arrived.astype(jnp.float32), down_node.astype(jnp.float32))
    onehot = (picked[:, :, None] == jnp.arange(E_NODE, dtype=jnp.int32)[None, None, :]).astype(jnp.float32)
    raw_grad = jnp.sum(onehot[:, :, :, None] * raw_all[:, None, :, :], axis=2)
    gate_saved = gate_stored.astype(jnp.float32)
    up_saved = up_stored.astype(jnp.float32)
    gate_sigmoid = jax.nn.sigmoid(gate_saved)
    activated = gate_saved * gate_sigmoid
    hidden = activated * up_saved
    router_slot = jnp.sum(hidden * raw_grad, axis=2).astype(jnp.bfloat16)
    hidden_grad = weight_row[:, :, None] * raw_grad
    gate_grad = (hidden_grad * up_saved * gate_sigmoid * (1.0 + gate_saved * (1.0 - gate_sigmoid))).astype(jnp.bfloat16)
    up_grad = (hidden_grad * activated).astype(jnp.bfloat16)
    gate_spread = jnp.sum(onehot[:, :, :, None] * gate_grad.astype(jnp.float32)[:, :, None, :], axis=1)
    up_spread = jnp.sum(onehot[:, :, :, None] * up_grad.astype(jnp.float32)[:, :, None, :], axis=1)
    back_gate = jnp.einsum("sef,edf->sd", gate_spread, gate_node.astype(jnp.float32))
    back_up = jnp.einsum("sef,edf->sd", up_spread, up_node.astype(jnp.float32))
    back_rows = (back_gate + back_up).astype(jnp.bfloat16)
    return back_rows, router_slot


def reference(out_grad, node_pick, expert_pick, pick_weight, gate_weight, up_weight, down_weight, saved_gate, saved_up):
    arrival_index = arrival(node_pick)
    flat_index = arrival_index.reshape(-1)
    token_rows = jnp.repeat(out_grad, GROUPS, axis=0)
    arrived = jnp.zeros((NODES * SLOTS, D), jnp.bfloat16).at[flat_index].set(token_rows).reshape(NODES, SLOTS, D)
    picked = jnp.zeros((NODES * SLOTS, PICKS), jnp.int32).at[flat_index].set(expert_pick.reshape(-1, PICKS).astype(jnp.int32)).reshape(NODES, SLOTS, PICKS)
    weight_rows = jnp.zeros((NODES * SLOTS, PICKS), jnp.float32).at[flat_index].set(pick_weight.reshape(-1, PICKS).astype(jnp.float32)).reshape(NODES, SLOTS, PICKS)
    back_rows, router_slot = lax.map(node_backward, (arrived, picked, weight_rows, gate_weight, up_weight, down_weight, saved_gate, saved_up))
    back_flat = back_rows.reshape(NODES * SLOTS, D)
    gathered = back_flat[flat_index].astype(jnp.float32).reshape(TOKENS, GROUPS, D)
    input_grad = jnp.sum(gathered, axis=1).astype(jnp.bfloat16)
    router_grad = router_slot.reshape(NODES * SLOTS, PICKS)[flat_index].reshape(TOKENS, GROUPS, PICKS)
    return input_grad, router_grad
```

```python
import functools

import jax
import jax.numpy as jnp
from jax import lax
from jax.experimental import pallas as pl
from jax.experimental.pallas import tpu as pltpu
from jax.sharding import PartitionSpec as P

BF16 = jnp.bfloat16
F32 = jnp.float32
LANES = 128
FOLD = 4
VMEM_LIMIT = 40 * 1024 * 1024


def round_up(value, unit):
    return -(-value // unit) * unit


def nn(a, b):
    return lax.dot_general(a, b, (((1,), (0,)), ((), ())), preferred_element_type=F32)


def nt(a, b):
    return lax.dot_general(a, b, (((1,), (1,)), ((), ())), preferred_element_type=F32)


def tn(a, b):
    return lax.dot_general(a, b, (((0,), (0,)), ((), ())), preferred_element_type=F32)


def iota(shape, axis):
    return lax.broadcasted_iota(jnp.int32, shape, axis)


def call(kernel, out_shape, **extra):
    return pl.pallas_call(
        kernel,
        out_shape=out_shape,
        compiler_params=pltpu.CompilerParams(vmem_limit_bytes=VMEM_LIMIT),
        **extra,
    )


def pair_maps(pick, nodes):
    groups, tokens = pick.shape
    rows = nodes * FOLD
    node_of = iota((rows, tokens), 0) // FOLD
    hits = [(pick[g : g + 1, :] == node_of).astype(F32) for g in range(groups)]
    named = functools.reduce(jnp.add, hits)
    earlier = (iota((tokens, tokens), 0) < iota((tokens, tokens), 1)).astype(BF16)
    slot = nn(named.astype(BF16), earlier).astype(jnp.int32)
    return named, slot, hits


def placing(named, slot, piece):
    row = iota(named.shape, 0) % FOLD
    return jnp.where(slot == piece * FOLD + row, named, 0.0)


def prepare_kernel(pieces, pick_ref, expert_ref, weight_ref, rows_ref, out_ref):
    nodes = out_ref.shape[0]
    width, tokens = rows_ref.shape
    rows = nodes * FOLD
    pick = pick_ref[...]
    named, slot, hits = pair_maps(pick, nodes)
    expert = functools.reduce(
        jnp.add, [hit * expert_ref[g].astype(F32) for g, hit in enumerate(hits)]
    )
    weights = weight_ref[...].astype(F32)
    weight = functools.reduce(
        jnp.add, [hit * weights[g : g + 1, :] for g, hit in enumerate(hits)]
    )
    token_rows = rows_ref[...]
    spare = out_ref.shape[2] - pieces * width
    lane = iota((rows, spare), 1)
    meta = jnp.zeros((rows, spare), F32)
    parts = []
    for piece in range(pieces):
        place = placing(named, slot, piece)
        parts.append(nt(place.astype(BF16), token_rows))
        picked = jnp.sum(place * expert, axis=1, keepdims=True)
        scale = jnp.sum(place * weight, axis=1, keepdims=True)
        meta = jnp.where(lane == piece, picked, meta)
        meta = jnp.where(lane == pieces + piece, scale, meta)
    block = jnp.concatenate(parts + [meta], axis=1)
    out_ref[...] = block.reshape(nodes, FOLD, block.shape[1]).astype(BF16)


def factors_kernel(gate_ref, up_ref, out_ref):
    gate = gate_ref[...].astype(F32)
    up = up_ref[...].astype(F32)
    sig = jax.nn.sigmoid(gate)
    slots, units = gate.shape
    rest = jnp.zeros((out_ref.shape[1] - slots, units), F32)
    by_gate = up * sig * (1.0 + gate * (1.0 - sig))
    by_up = gate * sig
    out_ref[0] = jnp.concatenate([by_gate, rest], axis=0).astype(BF16)
    out_ref[1] = jnp.concatenate([by_up, rest], axis=0).astype(BF16)


def unfold_matrix(blocks, pieces, held):
    shape = (blocks * held, pieces * blocks * FOLD)
    row, column = iota(shape, 0), iota(shape, 1)
    slot = row % held
    source = (slot // FOLD) * (blocks * FOLD) + (row // held) * FOLD + slot % FOLD
    return jnp.where(jnp.logical_and(source == column, slot < pieces * FOLD), 1.0, 0.0).astype(BF16)


def raw_kernel(pieces, width, held, adds, which_ref, in_ref, down_ref, *refs):
    other_ref = refs[0] if adds else None
    out_ref, meta_ref = refs[-2:]
    blocks, units = out_ref.shape[0], out_ref.shape[2]
    folded = in_ref[:, 0].astype(F32).reshape(blocks * FOLD, in_ref.shape[3])
    base = pieces * width
    pad = 2 * LANES - width
    stacked = []
    for piece in range(pieces):
        columns = [
            folded[:, piece * width : (piece + 1) * width],
            folded[:, base + piece : base + piece + 1],
            folded[:, base + pieces + piece : base + pieces + piece + 1],
            jnp.zeros((blocks * FOLD, pad - 2), F32),
        ]
        stacked.append(jnp.concatenate(columns, axis=1))
    stacked = jnp.concatenate(stacked, axis=0).astype(BF16)
    rows = nn(unfold_matrix(blocks, pieces, held), stacked)
    arrived = rows[:, :width]
    meta = rows[:, width : width + 2]
    first = meta[:, 0:1] == 0.0
    zero = jnp.zeros_like(arrived)
    raw = nn(jnp.where(first, arrived, zero).astype(BF16), down_ref[0])
    raw = raw + nn(jnp.where(first, zero, arrived).astype(BF16), down_ref[1])
    raw = raw.reshape(blocks, held, units)
    if adds:
        raw = raw + other_ref[...].astype(F32)
    out_ref[...] = raw.astype(BF16)
    meta_ref[...] = meta


def hidden_kernel(parts_ref, gate_ref, up_ref, out_ref):
    blocks, held, units = parts_ref.shape
    total = parts_ref[0].astype(F32)
    for at in range(1, blocks):
        total = total + parts_ref[at].astype(F32)
    slots = gate_ref.shape[0]
    raw = total[:slots]
    gate = gate_ref[...].astype(F32)
    up = up_ref[...].astype(F32)
    hidden = gate * jax.nn.sigmoid(gate) * up
    router = jnp.sum(hidden * raw, axis=1, keepdims=True)
    diagonal = iota((slots, units), 0) == iota((slots, units), 1)
    router_row = jnp.sum(jnp.where(diagonal, router, 0.0), axis=0, keepdims=True)
    rest = jnp.zeros((held - slots - 1, units), F32)
    block = jnp.concatenate([raw, router_row, rest], axis=0).astype(BF16)
    for at in range(blocks):
        out_ref[at] = block


def back_kernel(pieces, width, merges, which_ref, raw_ref, factor_ref, meta_ref, gate_ref, up_ref, *refs):
    blocks, held, units = raw_ref.shape
    out_ref = refs[-1]
    slots = pieces * FOLD
    raw = raw_ref[...].astype(F32)
    by_gate = (raw * factor_ref[:, 0, 0].astype(F32)).astype(BF16).reshape(blocks * held, units)
    by_up = (raw * factor_ref[:, 0, 1].astype(F32)).astype(BF16).reshape(blocks * held, units)
    meta = meta_ref[...]
    first = meta[:, 0:1] == 0.0
    back = jnp.where(
        first,
        nt(by_gate, gate_ref[0]) + nt(by_up, up_ref[0]),
        nt(by_gate, gate_ref[1]) + nt(by_up, up_ref[1]),
    )
    back = (back * meta[:, 1:2]).astype(BF16)
    folded = tn(unfold_matrix(blocks, pieces, held), back)
    rows = blocks * FOLD
    parts = [folded[piece * rows : (piece + 1) * rows] for piece in range(pieces)]
    router = raw[:, slots, :LANES].astype(BF16)
    spread = (iota((rows, blocks), 0) // FOLD == iota((rows, blocks), 1)).astype(F32).astype(BF16)
    router = nn(spread, router)
    kept = jnp.logical_and(
        iota((rows, LANES), 1) % FOLD == iota((rows, LANES), 0) % FOLD,
        iota((rows, LANES), 1) < slots,
    )
    router = jnp.where(kept, router, 0.0).astype(BF16)
    spare = out_ref.shape[-1] - pieces * width
    gather = (iota((LANES, spare), 0) // FOLD == iota((LANES, spare), 1)).astype(F32).astype(BF16)
    parts.append(nn(router, gather))
    block = jnp.concatenate(parts, axis=1)
    block = block.reshape(blocks, FOLD, block.shape[1]).astype(BF16)
    if merges:
        which = which_ref[0]
        out_ref[:, which] = block
        out_ref[:, 1 - which] = refs[0][...]
    else:
        out_ref[...] = block


def finish_kernel(pieces, width, in_ref, pick_ref, grad_ref, router_ref):
    nodes = in_ref.shape[0]
    pick = pick_ref[...]
    groups, tokens = pick.shape
    named, slot, hits = pair_maps(pick, nodes)
    rows = in_ref[...].astype(F32).reshape(nodes * FOLD, in_ref.shape[2])
    base = pieces * width
    total = jnp.zeros((width, tokens), F32)
    routed = jnp.zeros((nodes * FOLD, tokens), F32)
    for piece in range(pieces):
        place = placing(named, slot, piece)
        total = total + tn(
            rows[:, piece * width : (piece + 1) * width].astype(BF16), place.astype(BF16)
        )
        routed = routed + place * rows[:, base + piece : base + piece + 1]
    grad_ref[...] = total.astype(BF16)
    router = [jnp.sum(routed * hit, axis=0, keepdims=True) for hit in hits]
    router_ref[...] = jnp.concatenate(router, axis=0).astype(BF16)


def per_device(
    out_grad,
    node_pick,
    expert_pick,
    pick_weight,
    gate_weight,
    up_weight,
    down_weight,
    saved_gate,
    saved_up,
):
    nodes = lax.axis_size("node")
    local_count = lax.axis_size("local")
    tokens, width = out_grad.shape
    groups = node_pick.shape[1]
    experts, units = gate_weight.shape[1], gate_weight.shape[3]
    slots = saved_gate.shape[1]
    chips = local_count // 2
    pieces = slots // FOLD
    held = round_up(slots + 1, 8)
    block = round_up(pieces * width + 2 * pieces, LANES)
    core = (lax.axis_index("local") % 2).astype(jnp.int32)
    mine = core.reshape(1)
    other = 1 - mine
    same_core = [[2 * chip + c for chip in range(chips)] for c in range(2)]
    swap = [(at, at ^ 1) for at in range(local_count)]

    pick = node_pick.T
    gate_saved = saved_gate.reshape(slots, units)
    up_saved = saved_up.reshape(slots, units)
    down = jnp.swapaxes(down_weight[0], 1, 2)

    factors = call(factors_kernel, jax.ShapeDtypeStruct((2, held, units), BF16))(
        gate_saved, up_saved
    )
    factors = lax.all_gather(factors, "local", axis=0, tiled=False)
    factors = factors.reshape(chips, 2, 2, held, units)

    sent = call(
        functools.partial(prepare_kernel, pieces),
        jax.ShapeDtypeStruct((nodes, FOLD, block), BF16),
    )(pick, jnp.transpose(expert_pick, (1, 2, 0)), pick_weight[:, :, 0].T, out_grad.T)
    arrived = lax.all_to_all(sent, "node", split_axis=0, concat_axis=0, tiled=True)
    arrived = arrived.reshape(nodes // 2, 2, FOLD, block)

    def whole(shape):
        return pl.BlockSpec(shape, lambda i, which: (0,) * len(shape))

    def raw_part(which, received):
        adds = received is not None
        half = nodes // 2
        grid_spec = pltpu.PrefetchScalarGridSpec(
            num_scalar_prefetch=1,
            grid=(1,),
            in_specs=[
                pl.BlockSpec((half, 1, FOLD, block), lambda i, which: (0, which[0], 0, 0)),
                whole(down.shape),
            ]
            + ([whole((half, held, units))] if adds else []),
            out_specs=[whole((half, held, units)), whole((half * held, 2))],
        )
        return call(
            functools.partial(raw_kernel, pieces, width, held, adds),
            (
                jax.ShapeDtypeStruct((half, held, units), BF16),
                jax.ShapeDtypeStruct((half * held, 2), F32),
            ),
            grid_spec=grid_spec,
        )(which, arrived, down, *([received] if adds else []))

    theirs, other_meta = raw_part(other, None)
    received = lax.ppermute(theirs, "local", swap)
    partial, mine_meta = raw_part(mine, received)
    parts = lax.all_to_all(
        partial, "local", split_axis=0, concat_axis=0, axis_index_groups=same_core, tiled=True
    )
    spread = call(hidden_kernel, jax.ShapeDtypeStruct((chips, held, units), BF16))(
        parts, gate_saved, up_saved
    )
    raw_mine = lax.all_to_all(
        spread, "local", split_axis=0, concat_axis=0, axis_index_groups=same_core, tiled=True
    )
    raw_other = lax.ppermute(raw_mine, "local", swap)

    def back_part(which, raw, meta, done):
        merges = done is not None
        half = nodes // 2
        shape = (half, 2, FOLD, block) if merges else (half, FOLD, block)
        grid_spec = pltpu.PrefetchScalarGridSpec(
            num_scalar_prefetch=1,
            grid=(1,),
            in_specs=[
                whole((half, held, units)),
                pl.BlockSpec(
                    (half, 1, 2, held, units), lambda i, which: (0, which[0], 0, 0, 0)
                ),
                whole(meta.shape),
                whole((experts, width, units)),
                whole((experts, width, units)),
            ]
            + ([whole(done.shape)] if merges else []),
            out_specs=whole(shape),
        )
        return call(
            functools.partial(back_kernel, pieces, width, merges),
            jax.ShapeDtypeStruct(shape, BF16),
            grid_spec=grid_spec,
        )(which, raw, factors, meta, gate_weight[0], up_weight[0], *([done] if merges else []))

    back = back_part(mine, raw_mine, mine_meta, None)
    back = back_part(other, raw_other, other_meta, back)
    back = back.reshape(nodes, FOLD, block)
    returned = lax.all_to_all(back, "node", split_axis=0, concat_axis=0, tiled=True)
    grad, router = call(
        functools.partial(finish_kernel, pieces, width),
        (
            jax.ShapeDtypeStruct((width, tokens), BF16),
            jax.ShapeDtypeStruct((groups, tokens), BF16),
        ),
    )(returned, pick)
    return grad.T, router.T.reshape(tokens, groups, 1)


def solution(mesh):
    return jax.shard_map(
        per_device,
        mesh=mesh,
        in_specs=(
            P("node", "local"),
            P("node", None),
            P("node", None, None),
            P("node", None, None),
            P("node", None, "local", None),
            P("node", None, "local", None),
            P("node", None, None, "local"),
            P("node", "local", None, None),
            P("node", "local", None, None),
        ),
        out_specs=(P("node", "local"), P("node", None, None)),
        check_vma=False,
    )
```

```python
import functools

import jax
import jax.numpy as jnp
from jax import lax
from jax.experimental import pallas as pl
from jax.experimental.pallas import tpu as pltpu
from jax.sharding import PartitionSpec as P

BF16 = jnp.bfloat16
F32 = jnp.float32
LANES = 128
FOLD = 4
VMEM_LIMIT = 32 * 1024 * 1024
VMEM_MOST = 58 * 1024 * 1024
VMEM_BACK = 48 * 1024 * 1024


def round_up(value, unit):
    return -(-value // unit) * unit


def nn(a, b):
    return lax.dot_general(a, b, (((1,), (0,)), ((), ())), preferred_element_type=F32)


def nt(a, b):
    return lax.dot_general(a, b, (((1,), (1,)), ((), ())), preferred_element_type=F32)


def tn(a, b):
    return lax.dot_general(a, b, (((0,), (0,)), ((), ())), preferred_element_type=F32)


def iota(shape, axis):
    return lax.broadcasted_iota(jnp.int32, shape, axis)


def call(kernel, out_shape, limit=VMEM_LIMIT, **extra):
    return pl.pallas_call(
        kernel,
        out_shape=out_shape,
        compiler_params=pltpu.CompilerParams(vmem_limit_bytes=limit),
        **extra,
    )


def pair_maps(pick, nodes):
    groups, tokens = pick.shape
    rows = nodes * FOLD
    node_of = iota((rows, tokens), 0) // FOLD
    hits = [(pick[g : g + 1, :] == node_of).astype(F32) for g in range(groups)]
    named = functools.reduce(jnp.add, hits)
    earlier = (iota((tokens, tokens), 0) < iota((tokens, tokens), 1)).astype(BF16)
    slot = nn(named.astype(BF16), earlier).astype(jnp.int32)
    return named, slot, hits


def placing(named, slot, piece):
    row = iota(named.shape, 0) % FOLD
    return jnp.where(slot == piece * FOLD + row, named, 0.0)


def fetch(copies):
    for copy in copies:
        copy.start()


def pack(rows, slots):
    tiles = rows.shape[-1] // LANES
    axis = rows.ndim - 2
    pieces = [
        rows[..., :slots, tile * LANES : (tile + 1) * LANES] for tile in range(tiles)
    ]
    return [jnp.concatenate(pieces[at : at + 4], axis=axis) for at in range(0, tiles, 4)]


def prepare_kernel(
    pieces,
    pick_hbm,
    expert_hbm,
    weight_hbm,
    rows_hbm,
    gate_hbm,
    up_hbm,
    out_ref,
    factor_ref,
    pick_ref,
    expert_ref,
    weight_ref,
    rows_ref,
    gate_ref,
    up_ref,
    sems,
):
    pairs = [
        (pick_hbm, pick_ref),
        (expert_hbm, expert_ref),
        (weight_hbm, weight_ref),
        (rows_hbm, rows_ref),
        (gate_hbm, gate_ref),
        (up_hbm, up_ref),
    ]
    copies = [
        pltpu.make_async_copy(source, target, sems.at[at])
        for at, (source, target) in enumerate(pairs)
    ]
    fetch(copies)
    nodes = out_ref.shape[0]
    width, tokens = rows_ref.shape
    rows = nodes * FOLD
    for copy in copies[:4]:
        copy.wait()
    pick = pick_ref[...]
    named, slot, hits = pair_maps(pick, nodes)
    expert = functools.reduce(
        jnp.add, [hit * expert_ref[g].astype(F32) for g, hit in enumerate(hits)]
    )
    weights = weight_ref[...].astype(F32)
    weight = functools.reduce(
        jnp.add, [hit * weights[g : g + 1, :] for g, hit in enumerate(hits)]
    )
    token_rows = rows_ref[...]
    spare = out_ref.shape[2] - pieces * width
    lane = iota((rows, spare), 1)
    meta = jnp.zeros((rows, spare), F32)
    parts = []
    for piece in range(pieces):
        place = placing(named, slot, piece)
        parts.append(nt(place.astype(BF16), token_rows))
        picked = jnp.sum(place * expert, axis=1, keepdims=True)
        scale = jnp.sum(place * weight, axis=1, keepdims=True)
        meta = jnp.where(lane == piece, picked, meta)
        meta = jnp.where(lane == pieces + piece, scale, meta)
    block = jnp.concatenate(parts + [meta], axis=1)
    out_ref[...] = block.reshape(nodes, FOLD, block.shape[1]).astype(BF16)
    for copy in copies[4:]:
        copy.wait()
    gate = gate_ref[...].astype(F32)
    up = up_ref[...].astype(F32)
    sig = jax.nn.sigmoid(gate)
    slots = gate.shape[0]
    by_gate = up * sig * (1.0 + gate * (1.0 - sig))
    by_up = gate * sig
    for at, factor in enumerate((by_gate, by_up)):
        factor_ref[at] = jnp.concatenate(pack(factor, slots), axis=0).astype(BF16)


def keep_kernel(in_ref, after_ref, out_ref):
    out_ref[...] = in_ref[...]


def unfold_matrix(blocks, pieces, held):
    shape = (blocks * held, pieces * blocks * FOLD)
    row, column = iota(shape, 0), iota(shape, 1)
    slot = row % held
    source = (slot // FOLD) * (blocks * FOLD) + (row // held) * FOLD + slot % FOLD
    return jnp.where(jnp.logical_and(source == column, slot < pieces * FOLD), 1.0, 0.0).astype(BF16)


def raw_kernel(pieces, width, held, which_ref, in_ref, down_ref, out_ref, meta_ref):
    blocks = out_ref.shape[0]
    units = down_ref.shape[2]
    slots = pieces * FOLD
    folded = in_ref[:, which_ref[0]].astype(F32).reshape(blocks * FOLD, in_ref.shape[3])
    base = pieces * width
    pad = 2 * LANES - width
    stacked = []
    for piece in range(pieces):
        columns = [
            folded[:, piece * width : (piece + 1) * width],
            folded[:, base + piece : base + piece + 1],
            folded[:, base + pieces + piece : base + pieces + piece + 1],
            jnp.zeros((blocks * FOLD, pad - 2), F32),
        ]
        stacked.append(jnp.concatenate(columns, axis=1))
    stacked = jnp.concatenate(stacked, axis=0).astype(BF16)
    rows = nn(unfold_matrix(blocks, pieces, held), stacked)
    arrived = rows[:, :width]
    meta = rows[:, width : width + 2]
    first = meta[:, 0:1] == 0.0
    zero = jnp.zeros_like(arrived)
    raw = nn(jnp.where(first, arrived, zero).astype(BF16), down_ref[0])
    raw = raw + nn(jnp.where(first, zero, arrived).astype(BF16), down_ref[1])
    parts = pack(raw.reshape(blocks, held, units), slots)
    rows = parts[0].shape[1]
    for at, part in enumerate(parts):
        out_ref[:, at * rows : (at + 1) * rows, :] = part.astype(out_ref.dtype)
    meta_ref[...] = meta


def add_kernel(mine_ref, other_ref, out_ref):
    out_ref[...] = (mine_ref[...] + other_ref[...].astype(F32)).astype(BF16)


def hidden_kernel(parts_ref, gate_ref, up_ref, out_ref):
    blocks, rows, _ = parts_ref.shape
    total = parts_ref[0].astype(F32)
    for at in range(1, blocks):
        total = total + parts_ref[at].astype(F32)
    slots, units = gate_ref.shape
    raw = jnp.concatenate(
        [total[tile * slots : (tile + 1) * slots] for tile in range(units // LANES)], axis=1
    )
    gate = gate_ref[...].astype(F32)
    up = up_ref[...].astype(F32)
    hidden = gate * jax.nn.sigmoid(gate) * up
    router = jnp.sum(hidden * raw, axis=1, keepdims=True)
    diagonal = iota((slots, LANES), 0) == iota((slots, LANES), 1)
    router_row = jnp.sum(jnp.where(diagonal, router, 0.0), axis=0, keepdims=True)
    spare = out_ref.shape[1] - rows
    extra = jnp.where(iota((spare, LANES), 0) == 0, router_row, 0.0)
    block = jnp.concatenate([total, extra], axis=0).astype(BF16)
    for at in range(blocks):
        out_ref[at] = block


def back_kernel(
    pieces, width, held, merges, which_ref, raw_ref, meta_hbm, gate_ref, up_ref, *refs
):
    blocks = raw_ref.shape[0]
    units = gate_ref.shape[2]
    tiles = units // LANES
    slots = pieces * FOLD
    which = which_ref[0]
    if merges:
        factor_ref, done_ref, out_ref, meta_ref, sems = refs
        copies = [pltpu.make_async_copy(meta_hbm, meta_ref, sems.at[0])]
    else:
        factor_hbm, out_ref, later_ref, factor_ref, meta_ref, sems = refs
        copies = [
            pltpu.make_async_copy(meta_hbm, meta_ref, sems.at[0]),
            pltpu.make_async_copy(factor_hbm.at[:, which], factor_ref, sems.at[1]),
            pltpu.make_async_copy(factor_hbm.at[:, 1 - which], later_ref, sems.at[2]),
        ]
    fetch(copies)
    unfold = unfold_matrix(blocks, pieces, held)
    raw = raw_ref[...].astype(F32)
    for copy in copies[:2]:
        copy.wait()
    spare = jnp.zeros((blocks, held - slots + 4, LANES), F32)

    def spread(at):
        packed = raw[:, : tiles * slots] * factor_ref[:, at].astype(F32)
        packed = jnp.concatenate([packed, spare], axis=1)
        parts = [
            packed[:, tile * slots : tile * slots + held].reshape(blocks * held, LANES)
            for tile in range(tiles)
        ]
        return jnp.concatenate(parts, axis=1).astype(BF16)

    by_gate = spread(0)
    by_up = spread(1)
    meta = meta_ref[...]
    first = meta[:, 0:1] == 0.0
    back = jnp.where(
        first,
        nt(by_gate, gate_ref[0]) + nt(by_up, up_ref[0]),
        nt(by_gate, gate_ref[1]) + nt(by_up, up_ref[1]),
    )
    back = (back * meta[:, 1:2]).astype(BF16)
    folded = tn(unfold, back)
    rows = blocks * FOLD
    parts = [folded[piece * rows : (piece + 1) * rows] for piece in range(pieces)]
    router = raw[:, tiles * slots].astype(BF16)
    repeat = (iota((rows, blocks), 0) // FOLD == iota((rows, blocks), 1)).astype(F32).astype(BF16)
    router = nn(repeat, router)
    kept = jnp.logical_and(
        iota((rows, LANES), 1) % FOLD == iota((rows, LANES), 0) % FOLD,
        iota((rows, LANES), 1) < slots,
    )
    router = jnp.where(kept, router, 0.0).astype(BF16)
    lanes_left = out_ref.shape[-1] - pieces * width
    gather = iota((LANES, lanes_left), 0) // FOLD == iota((LANES, lanes_left), 1)
    parts.append(nn(router, gather.astype(F32).astype(BF16)))
    block = jnp.concatenate(parts, axis=1)
    block = block.reshape(blocks, FOLD, block.shape[1]).astype(BF16)
    if merges:
        out_ref[:, which] = block
        out_ref[:, 1 - which] = done_ref[...]
    else:
        out_ref[...] = block
    for copy in copies[2:]:
        copy.wait()


def finish_kernel(pieces, width, in_ref, pick_ref, grad_ref, router_ref):
    nodes = in_ref.shape[0]
    pick = pick_ref[...]
    groups, tokens = pick.shape
    named, slot, hits = pair_maps(pick, nodes)
    rows = in_ref[...].astype(F32).reshape(nodes * FOLD, in_ref.shape[2])
    base = pieces * width
    total = jnp.zeros((width, tokens), F32)
    routed = jnp.zeros((nodes * FOLD, tokens), F32)
    for piece in range(pieces):
        place = placing(named, slot, piece)
        total = total + tn(
            rows[:, piece * width : (piece + 1) * width].astype(BF16), place.astype(BF16)
        )
        routed = routed + place * rows[:, base + piece : base + piece + 1]
    grad_ref[...] = total.astype(BF16)
    router = [jnp.sum(routed * hit, axis=0, keepdims=True) for hit in hits]
    router_ref[...] = jnp.concatenate(router, axis=0).astype(BF16)


def per_device(
    out_grad,
    node_pick,
    expert_pick,
    pick_weight,
    gate_weight,
    up_weight,
    down_weight,
    saved_gate,
    saved_up,
):
    nodes = lax.axis_size("node")
    local_count = lax.axis_size("local")
    tokens, width = out_grad.shape
    groups = node_pick.shape[1]
    experts, units = gate_weight.shape[1], gate_weight.shape[3]
    slots = saved_gate.shape[1]
    chips = local_count // 2
    pieces = slots // FOLD
    tiles = units // LANES
    half = nodes // 2
    held = round_up(slots, 8)
    packed = tiles * slots
    block = round_up(pieces * width + 2 * pieces, LANES)
    core = (lax.axis_index("local") % 2).astype(jnp.int32)
    mine = core.reshape(1)
    other = 1 - mine
    same_core = [[2 * chip + c for chip in range(chips)] for c in range(2)]
    swap = [(at, at ^ 1) for at in range(local_count)]

    pick = node_pick.T
    gate_saved = saved_gate.reshape(slots, units)
    up_saved = saved_up.reshape(slots, units)
    down = jnp.swapaxes(down_weight[0], 1, 2)
    hbm = pl.BlockSpec(memory_space=pltpu.HBM)
    vmem = pl.BlockSpec(memory_space=pltpu.VMEM)
    smem = pl.BlockSpec(memory_space=pltpu.SMEM)

    sent, factors = call(
        functools.partial(prepare_kernel, pieces),
        (
            jax.ShapeDtypeStruct((nodes, FOLD, block), BF16),
            jax.ShapeDtypeStruct((2, packed, LANES), BF16),
        ),
        limit=VMEM_MOST,
        in_specs=[hbm] * 6,
        out_specs=[vmem] * 2,
        scratch_shapes=[
            pltpu.VMEM((groups, tokens), jnp.int32),
            pltpu.VMEM((groups, 1, tokens), jnp.int32),
            pltpu.VMEM((groups, tokens), BF16),
            pltpu.VMEM((width, tokens), BF16),
            pltpu.VMEM((slots, units), BF16),
            pltpu.VMEM((slots, units), BF16),
            pltpu.SemaphoreType.DMA((6,)),
        ],
    )(
        pick,
        jnp.transpose(expert_pick, (1, 2, 0)),
        pick_weight[:, :, 0].T,
        out_grad.T,
        gate_saved,
        up_saved,
    )
    down = call(
        keep_kernel,
        jax.ShapeDtypeStruct(down.shape, BF16),
        in_specs=[vmem, hbm],
        out_specs=vmem,
    )(down, factors)
    factors = lax.all_gather(factors, "local", axis=0, tiled=False)
    factors = factors.reshape(chips, 2, 2, packed, LANES)
    arrived = lax.all_to_all(sent, "node", split_axis=0, concat_axis=0, tiled=True)
    arrived = arrived.reshape(half, 2, FOLD, block)

    def raw_part(which, dtype):
        return call(
            functools.partial(raw_kernel, pieces, width, held),
            (
                jax.ShapeDtypeStruct((half, packed, LANES), dtype),
                jax.ShapeDtypeStruct((half * held, 2), F32),
            ),
            in_specs=[smem, vmem, vmem],
            out_specs=[vmem, vmem],
        )(which, arrived, down)

    theirs, other_meta = raw_part(other, BF16)
    received = lax.ppermute(theirs, "local", swap)
    partial, mine_meta = raw_part(mine, F32)
    partial = call(add_kernel, jax.ShapeDtypeStruct((half, packed, LANES), BF16))(
        partial, received
    )
    parts = lax.all_to_all(
        partial, "local", split_axis=0, concat_axis=0, axis_index_groups=same_core, tiled=True
    )
    spread = call(
        hidden_kernel, jax.ShapeDtypeStruct((chips, packed + 16, LANES), BF16)
    )(parts, gate_saved, up_saved)
    raw_mine = lax.all_to_all(
        spread, "local", split_axis=0, concat_axis=0, axis_index_groups=same_core, tiled=True
    )
    raw_other = lax.ppermute(raw_mine, "local", swap)

    factor_shape = (half, 2, packed, LANES)
    meta_shape = (half * held, 2)
    back, later = call(
        functools.partial(back_kernel, pieces, width, held, False),
        (
            jax.ShapeDtypeStruct((half, FOLD, block), BF16),
            jax.ShapeDtypeStruct(factor_shape, BF16),
        ),
        limit=VMEM_BACK,
        in_specs=[smem, vmem, hbm, vmem, vmem, hbm],
        out_specs=[vmem, vmem],
        scratch_shapes=[
            pltpu.VMEM(factor_shape, BF16),
            pltpu.VMEM(meta_shape, F32),
            pltpu.SemaphoreType.DMA((3,)),
        ],
    )(mine, raw_mine, mine_meta, gate_weight[0], up_weight[0], factors)
    back = call(
        functools.partial(back_kernel, pieces, width, held, True),
        jax.ShapeDtypeStruct((half, 2, FOLD, block), BF16),
        in_specs=[smem, vmem, hbm, vmem, vmem, vmem, vmem],
        out_specs=vmem,
        scratch_shapes=[pltpu.VMEM(meta_shape, F32), pltpu.SemaphoreType.DMA((1,))],
    )(other, raw_other, other_meta, gate_weight[0], up_weight[0], later, back)
    back = back.reshape(nodes, FOLD, block)
    returned = lax.all_to_all(back, "node", split_axis=0, concat_axis=0, tiled=True)
    grad, router = call(
        functools.partial(finish_kernel, pieces, width),
        (
            jax.ShapeDtypeStruct((width, tokens), BF16),
            jax.ShapeDtypeStruct((groups, tokens), BF16),
        ),
    )(returned, pick)
    return grad.T, router.T.reshape(tokens, groups, 1)


def solution(mesh):
    return jax.shard_map(
        per_device,
        mesh=mesh,
        in_specs=(
            P("node", "local"),
            P("node", None),
            P("node", None, None),
            P("node", None, None),
            P("node", None, "local", None),
            P("node", None, "local", None),
            P("node", None, None, "local"),
            P("node", "local", None, None),
            P("node", "local", None, None),
        ),
        out_specs=(P("node", "local"), P("node", None, None)),
        check_vma=False,
    )
```

```python
import functools

import jax
import jax.numpy as jnp
from jax import lax
from jax.experimental import pallas as pl
from jax.experimental.pallas import tpu as pltpu
from jax.sharding import PartitionSpec as P

BF16 = jnp.bfloat16
F32 = jnp.float32
LANES = 128
FOLD = 4
VMEM_LIMIT = 32 * 1024 * 1024
VMEM_MOST = 58 * 1024 * 1024


def round_up(value, unit):
    return -(-value // unit) * unit


def nn(a, b):
    return lax.dot_general(a, b, (((1,), (0,)), ((), ())), preferred_element_type=F32)


def nt(a, b):
    return lax.dot_general(a, b, (((1,), (1,)), ((), ())), preferred_element_type=F32)


def tn(a, b):
    return lax.dot_general(a, b, (((0,), (0,)), ((), ())), preferred_element_type=F32)


def iota(shape, axis):
    return lax.broadcasted_iota(jnp.int32, shape, axis)


def call(kernel, out_shape, limit=VMEM_LIMIT, **extra):
    return pl.pallas_call(
        kernel,
        out_shape=out_shape,
        compiler_params=pltpu.CompilerParams(vmem_limit_bytes=limit),
        **extra,
    )


def pair_maps(pick, nodes):
    groups, tokens = pick.shape
    rows = nodes * FOLD
    node_of = iota((rows, tokens), 0) // FOLD
    hits = [(pick[g : g + 1, :] == node_of).astype(F32) for g in range(groups)]
    named = functools.reduce(jnp.add, hits)
    earlier = (iota((tokens, tokens), 0) < iota((tokens, tokens), 1)).astype(BF16)
    slot = nn(named.astype(BF16), earlier).astype(jnp.int32)
    return named, slot, hits


def placing(named, slot, piece):
    row = iota(named.shape, 0) % FOLD
    return jnp.where(slot == piece * FOLD + row, named, 0.0)


def fetch(copies):
    for copy in copies:
        copy.start()


def pack(rows, slots):
    tiles = rows.shape[-1] // LANES
    axis = rows.ndim - 2
    pieces = [
        rows[..., :slots, tile * LANES : (tile + 1) * LANES] for tile in range(tiles)
    ]
    return [jnp.concatenate(pieces[at : at + 4], axis=axis) for at in range(0, tiles, 4)]


def prepare_kernel(
    pieces,
    pick_hbm,
    expert_hbm,
    weight_hbm,
    rows_hbm,
    out_ref,
    pick_ref,
    expert_ref,
    weight_ref,
    rows_ref,
    sems,
):
    pairs = [
        (pick_hbm, pick_ref),
        (expert_hbm, expert_ref),
        (weight_hbm, weight_ref),
        (rows_hbm, rows_ref),
    ]
    copies = [
        pltpu.make_async_copy(source, target, sems.at[at])
        for at, (source, target) in enumerate(pairs)
    ]
    fetch(copies)
    nodes = out_ref.shape[0]
    width, tokens = rows_ref.shape
    rows = nodes * FOLD
    for copy in copies:
        copy.wait()
    pick = pick_ref[...]
    named, slot, hits = pair_maps(pick, nodes)
    expert = functools.reduce(
        jnp.add, [hit * expert_ref[g].astype(F32) for g, hit in enumerate(hits)]
    )
    weights = weight_ref[...].astype(F32)
    weight = functools.reduce(
        jnp.add, [hit * weights[g : g + 1, :] for g, hit in enumerate(hits)]
    )
    token_rows = rows_ref[...]
    spare = out_ref.shape[2] - pieces * width
    lane = iota((rows, spare), 1)
    meta = jnp.zeros((rows, spare), F32)
    parts = []
    for piece in range(pieces):
        place = placing(named, slot, piece)
        parts.append(nt(place.astype(BF16), token_rows))
        picked = jnp.sum(place * expert, axis=1, keepdims=True)
        scale = jnp.sum(place * weight, axis=1, keepdims=True)
        meta = jnp.where(lane == piece, picked, meta)
        meta = jnp.where(lane == pieces + piece, scale, meta)
    block = jnp.concatenate(parts + [meta], axis=1)
    out_ref[...] = block.reshape(nodes, FOLD, block.shape[1]).astype(BF16)

def keep_kernel(in_ref, after_ref, out_ref):
    out_ref[...] = in_ref[...]


def unfold_matrix(blocks, pieces, held):
    shape = (blocks * held, pieces * blocks * FOLD)
    row, column = iota(shape, 0), iota(shape, 1)
    slot = row % held
    source = (slot // FOLD) * (blocks * FOLD) + (row // held) * FOLD + slot % FOLD
    return jnp.where(jnp.logical_and(source == column, slot < pieces * FOLD), 1.0, 0.0).astype(BF16)


def raw_kernel(pieces, width, held, which_ref, in_ref, down_ref, out_ref):
    blocks = out_ref.shape[0]
    units = down_ref.shape[2]
    slots = pieces * FOLD
    folded = in_ref[:, which_ref[0]].astype(F32).reshape(blocks * FOLD, in_ref.shape[3])
    base = pieces * width
    spare = jnp.zeros((blocks * FOLD, 2 * LANES - width - 1), F32)
    stacked = []
    for piece in range(pieces):
        columns = [
            folded[:, piece * width : (piece + 1) * width],
            folded[:, base + piece : base + piece + 1],
            spare,
        ]
        stacked.append(jnp.concatenate(columns, axis=1))
    stacked = jnp.concatenate(stacked, axis=0).astype(BF16)
    rows = nn(unfold_matrix(blocks, pieces, held), stacked)
    arrived = rows[:, :width]
    first = rows[:, width : width + 1] == 0.0
    zero = jnp.zeros_like(arrived)
    raw = nn(jnp.where(first, arrived, zero).astype(BF16), down_ref[0])
    raw = raw + nn(jnp.where(first, zero, arrived).astype(BF16), down_ref[1])
    parts = pack(raw.reshape(blocks, held, units), slots)
    rows = parts[0].shape[1]
    for at, part in enumerate(parts):
        out_ref[:, at * rows : (at + 1) * rows, :] = part.astype(out_ref.dtype)


def add_kernel(mine_ref, other_ref, out_ref):
    out_ref[...] = (mine_ref[...] + other_ref[...].astype(F32)).astype(BF16)


def lanes_of(column):
    shape = (column.shape[0], LANES)
    return jnp.sum(jnp.where(iota(shape, 0) == iota(shape, 1), column, 0.0), axis=0, keepdims=True)


def hidden_kernel(pieces, width, at_ref, parts_ref, in_ref, gate_ref, up_ref, out_ref):
    blocks, packed, _ = parts_ref.shape
    total = parts_ref[0].astype(F32)
    for at in range(1, blocks):
        total = total + parts_ref[at].astype(F32)
    slots, units = gate_ref.shape
    raw = jnp.concatenate(
        [total[tile * slots : (tile + 1) * slots] for tile in range(units // LANES)], axis=1
    )
    own = in_ref[at_ref[0] >> 1, at_ref[0] & 1].astype(F32)
    base = pieces * width
    picked = jnp.concatenate(
        [own[:, base + at : base + at + 1] for at in range(pieces)], axis=0
    )
    base = base + pieces
    weight = jnp.concatenate(
        [own[:, base + at : base + at + 1] for at in range(pieces)], axis=0
    )
    gate = gate_ref[...].astype(F32)
    up = up_ref[...].astype(F32)
    sig = jax.nn.sigmoid(gate)
    active = gate * sig
    router = jnp.sum(active * up * raw, axis=1, keepdims=True)
    scaled = weight * raw
    by_gate = scaled * up * sig * (1.0 + gate * (1.0 - sig))
    by_up = scaled * active
    spare = out_ref.shape[1] - 2 * packed
    row = iota((spare, LANES), 0)
    extra = jnp.where(row == 0, lanes_of(router), jnp.where(row == 1, lanes_of(picked), 0.0))
    block = jnp.concatenate(pack(by_gate, slots) + pack(by_up, slots) + [extra], axis=0)
    block = block.astype(BF16)
    for at in range(blocks):
        out_ref[at] = block


def back_kernel(pieces, width, held, merges, which_ref, in_ref, gate_ref, up_ref, *refs):
    out_ref = refs[-1]
    blocks = in_ref.shape[0]
    units = gate_ref.shape[2]
    tiles = units // LANES
    slots = pieces * FOLD
    packed = tiles * slots
    unfold = unfold_matrix(blocks, pieces, held)
    block = in_ref[...].astype(F32)

    def spread(start):
        parts = [
            block[:, start + tile * slots : start + tile * slots + held].reshape(
                blocks * held, LANES
            )
            for tile in range(tiles)
        ]
        return jnp.concatenate(parts, axis=1).astype(BF16)

    by_gate = spread(0)
    by_up = spread(packed)
    shape = (blocks, held, LANES)
    picked = jnp.where(
        iota(shape, 1) == iota(shape, 2), block[:, 2 * packed + 1 : 2 * packed + 2], 0.0
    )
    picked = jnp.sum(picked, axis=2, keepdims=True).reshape(blocks * held, 1)
    back = jnp.where(
        picked == 0.0,
        nt(by_gate, gate_ref[0]) + nt(by_up, up_ref[0]),
        nt(by_gate, gate_ref[1]) + nt(by_up, up_ref[1]),
    )
    folded = tn(unfold, back.astype(BF16))
    rows = blocks * FOLD
    parts = [folded[piece * rows : (piece + 1) * rows] for piece in range(pieces)]
    router = block[:, 2 * packed].astype(BF16)
    repeat = (iota((rows, blocks), 0) // FOLD == iota((rows, blocks), 1)).astype(F32).astype(BF16)
    router = nn(repeat, router)
    kept = jnp.logical_and(
        iota((rows, LANES), 1) % FOLD == iota((rows, LANES), 0) % FOLD,
        iota((rows, LANES), 1) < slots,
    )
    router = jnp.where(kept, router, 0.0).astype(BF16)
    lanes_left = out_ref.shape[-1] - pieces * width
    gather = iota((LANES, lanes_left), 0) // FOLD == iota((LANES, lanes_left), 1)
    parts.append(nn(router, gather.astype(F32).astype(BF16)))
    sent = jnp.concatenate(parts, axis=1)
    sent = sent.reshape(blocks, FOLD, sent.shape[1]).astype(BF16)
    if merges:
        which = which_ref[0]
        out_ref[:, which] = sent
        out_ref[:, 1 - which] = refs[0][...]
    else:
        out_ref[...] = sent


def finish_kernel(pieces, width, in_ref, pick_ref, grad_ref, router_ref):
    nodes = in_ref.shape[0]
    pick = pick_ref[...]
    groups, tokens = pick.shape
    named, slot, hits = pair_maps(pick, nodes)
    rows = in_ref[...].astype(F32).reshape(nodes * FOLD, in_ref.shape[2])
    base = pieces * width
    total = jnp.zeros((width, tokens), F32)
    routed = jnp.zeros((nodes * FOLD, tokens), F32)
    for piece in range(pieces):
        place = placing(named, slot, piece)
        total = total + tn(
            rows[:, piece * width : (piece + 1) * width].astype(BF16), place.astype(BF16)
        )
        routed = routed + place * rows[:, base + piece : base + piece + 1]
    grad_ref[...] = total.astype(BF16)
    router = [jnp.sum(routed * hit, axis=0, keepdims=True) for hit in hits]
    router_ref[...] = jnp.concatenate(router, axis=0).astype(BF16)


def per_device(
    out_grad,
    node_pick,
    expert_pick,
    pick_weight,
    gate_weight,
    up_weight,
    down_weight,
    saved_gate,
    saved_up,
):
    nodes = lax.axis_size("node")
    local_count = lax.axis_size("local")
    tokens, width = out_grad.shape
    groups = node_pick.shape[1]
    experts, units = gate_weight.shape[1], gate_weight.shape[3]
    slots = saved_gate.shape[1]
    chips = local_count // 2
    pieces = slots // FOLD
    tiles = units // LANES
    half = nodes // 2
    held = round_up(slots, 8)
    packed = tiles * slots
    block = round_up(pieces * width + 2 * pieces, LANES)
    place = lax.axis_index("local").astype(jnp.int32)
    own = place.reshape(1)
    mine = own & 1
    other = 1 - mine
    same_core = [[2 * chip + c for chip in range(chips)] for c in range(2)]
    swap = [(at, at ^ 1) for at in range(local_count)]

    pick = node_pick.T
    gate_saved = saved_gate.reshape(slots, units)
    up_saved = saved_up.reshape(slots, units)
    down = jnp.swapaxes(down_weight[0], 1, 2)
    hbm = pl.BlockSpec(memory_space=pltpu.HBM)
    vmem = pl.BlockSpec(memory_space=pltpu.VMEM)
    smem = pl.BlockSpec(memory_space=pltpu.SMEM)

    sent = call(
        functools.partial(prepare_kernel, pieces),
        jax.ShapeDtypeStruct((nodes, FOLD, block), BF16),
        limit=VMEM_MOST,
        in_specs=[hbm] * 4,
        out_specs=vmem,
        scratch_shapes=[
            pltpu.VMEM((groups, tokens), jnp.int32),
            pltpu.VMEM((groups, 1, tokens), jnp.int32),
            pltpu.VMEM((groups, tokens), BF16),
            pltpu.VMEM((width, tokens), BF16),
            pltpu.SemaphoreType.DMA((4,)),
        ],
    )(pick, jnp.transpose(expert_pick, (1, 2, 0)), pick_weight[:, :, 0].T, out_grad.T)
    down = call(
        keep_kernel,
        jax.ShapeDtypeStruct(down.shape, BF16),
        in_specs=[vmem, hbm],
        out_specs=vmem,
    )(down, sent)
    arrived = lax.all_to_all(sent, "node", split_axis=0, concat_axis=0, tiled=True)
    arrived = arrived.reshape(half, 2, FOLD, block)

    def raw_part(which, dtype):
        return call(
            functools.partial(raw_kernel, pieces, width, held),
            jax.ShapeDtypeStruct((half, packed, LANES), dtype),
            in_specs=[smem, vmem, vmem],
            out_specs=vmem,
        )(which, arrived, down)

    theirs = raw_part(other, BF16)
    received = lax.ppermute(theirs, "local", swap)
    partial = raw_part(mine, F32)
    partial = call(add_kernel, jax.ShapeDtypeStruct((half, packed, LANES), BF16))(
        partial, received
    )
    parts = lax.all_to_all(
        partial, "local", split_axis=0, concat_axis=0, axis_index_groups=same_core, tiled=True
    )
    hidden = call(
        functools.partial(hidden_kernel, pieces, width),
        jax.ShapeDtypeStruct((chips, 2 * packed + 16, LANES), BF16),
        in_specs=[smem, vmem, vmem, vmem, vmem],
        out_specs=vmem,
    )(own, parts, arrived, gate_saved, up_saved)
    hidden_mine = lax.all_to_all(
        hidden, "local", split_axis=0, concat_axis=0, axis_index_groups=same_core, tiled=True
    )
    hidden_other = lax.ppermute(hidden_mine, "local", swap)
    back = call(
        functools.partial(back_kernel, pieces, width, held, False),
        jax.ShapeDtypeStruct((half, FOLD, block), BF16),
        in_specs=[smem, vmem, vmem, vmem],
        out_specs=vmem,
    )(mine, hidden_mine, gate_weight[0], up_weight[0])
    back = call(
        functools.partial(back_kernel, pieces, width, held, True),
        jax.ShapeDtypeStruct((half, 2, FOLD, block), BF16),
        in_specs=[smem, vmem, vmem, vmem, vmem],
        out_specs=vmem,
    )(other, hidden_other, gate_weight[0], up_weight[0], back)
    back = back.reshape(nodes, FOLD, block)
    returned = lax.all_to_all(back, "node", split_axis=0, concat_axis=0, tiled=True)
    grad, router = call(
        functools.partial(finish_kernel, pieces, width),
        (
            jax.ShapeDtypeStruct((width, tokens), BF16),
            jax.ShapeDtypeStruct((groups, tokens), BF16),
        ),
    )(returned, pick)
    return grad.T, router.T.reshape(tokens, groups, 1)


def solution(mesh):
    return jax.shard_map(
        per_device,
        mesh=mesh,
        in_specs=(
            P("node", "local"),
            P("node", None),
            P("node", None, None),
            P("node", None, None),
            P("node", None, "local", None),
            P("node", None, "local", None),
            P("node", None, None, "local"),
            P("node", "local", None, None),
            P("node", "local", None, None),
        ),
        out_specs=(P("node", "local"), P("node", None, None)),
        check_vma=False,
    )
```

```python
import functools

import jax
import jax.numpy as jnp
from jax import lax
from jax.experimental import pallas as pl
from jax.experimental.pallas import tpu as pltpu
from jax.sharding import PartitionSpec as P

BF16 = jnp.bfloat16
F32 = jnp.float32
LANES = 128
FOLD = 4
VMEM_LIMIT = 32 * 1024 * 1024
CURVE = (0, 1, 5, 4, 8, 12, 13, 9, 10, 14, 15, 11, 7, 6, 2, 3)
VMEM_MOST = 58 * 1024 * 1024


def round_up(value, unit):
    return -(-value // unit) * unit


def nn(a, b):
    return lax.dot_general(a, b, (((1,), (0,)), ((), ())), preferred_element_type=F32)


def nt(a, b):
    return lax.dot_general(a, b, (((1,), (1,)), ((), ())), preferred_element_type=F32)


def tn(a, b):
    return lax.dot_general(a, b, (((0,), (0,)), ((), ())), preferred_element_type=F32)


def iota(shape, axis):
    return lax.broadcasted_iota(jnp.int32, shape, axis)


def call(kernel, out_shape, limit=VMEM_LIMIT, **extra):
    return pl.pallas_call(
        kernel,
        out_shape=out_shape,
        compiler_params=pltpu.CompilerParams(vmem_limit_bytes=limit),
        **extra,
    )


def chip_order(chips):
    return CURVE if chips == len(CURVE) else tuple(range(chips))


def pair_maps(pick, nodes, backwards):
    groups, tokens = pick.shape
    rows = nodes * FOLD
    node_of = iota((rows, tokens), 0) // FOLD
    if backwards:
        node_of = nodes - 1 - node_of
    hits = [(pick[g : g + 1, :] == node_of).astype(F32) for g in range(groups)]
    named = functools.reduce(jnp.add, hits)
    earlier = (iota((tokens, tokens), 0) < iota((tokens, tokens), 1)).astype(BF16)
    slot = nn(named.astype(BF16), earlier).astype(jnp.int32)
    return named, slot, hits


def placing(named, slot, piece):
    row = iota(named.shape, 0) % FOLD
    return jnp.where(slot == piece * FOLD + row, named, 0.0)


def fetch(copies):
    for copy in copies:
        copy.start()


def pack(rows, slots):
    tiles = rows.shape[-1] // LANES
    axis = rows.ndim - 2
    pieces = [
        rows[..., :slots, tile * LANES : (tile + 1) * LANES] for tile in range(tiles)
    ]
    return [jnp.concatenate(pieces[at : at + 4], axis=axis) for at in range(0, tiles, 4)]


def prepare_kernel(
    pieces,
    pick_hbm,
    expert_hbm,
    weight_hbm,
    rows_hbm,
    out_ref,
    pick_ref,
    expert_ref,
    weight_ref,
    rows_ref,
    sems,
):
    pairs = [
        (pick_hbm, pick_ref),
        (expert_hbm, expert_ref),
        (weight_hbm, weight_ref),
        (rows_hbm, rows_ref),
    ]
    copies = [
        pltpu.make_async_copy(source, target, sems.at[at])
        for at, (source, target) in enumerate(pairs)
    ]
    fetch(copies)
    nodes = out_ref.shape[0]
    width, tokens = rows_ref.shape
    rows = nodes * FOLD
    for copy in copies:
        copy.wait()
    pick = pick_ref[...]
    named, slot, hits = pair_maps(pick, nodes, True)
    expert = functools.reduce(
        jnp.add, [hit * expert_ref[g].astype(F32) for g, hit in enumerate(hits)]
    )
    weights = weight_ref[...].astype(F32)
    weight = functools.reduce(
        jnp.add, [hit * weights[g : g + 1, :] for g, hit in enumerate(hits)]
    )
    token_rows = rows_ref[...]
    spare = out_ref.shape[2] - pieces * width
    lane = iota((rows, spare), 1)
    meta = jnp.zeros((rows, spare), F32)
    parts = []
    for piece in range(pieces):
        place = placing(named, slot, piece)
        parts.append(nt(place.astype(BF16), token_rows))
        picked = jnp.sum(place * expert, axis=1, keepdims=True)
        scale = jnp.sum(place * weight, axis=1, keepdims=True)
        meta = jnp.where(lane == piece, picked, meta)
        meta = jnp.where(lane == pieces + piece, scale, meta)
    block = jnp.concatenate(parts + [meta], axis=1)
    out_ref[...] = block.reshape(nodes, FOLD, block.shape[1]).astype(BF16)

def keep_kernel(in_ref, after_ref, out_ref):
    out_ref[...] = in_ref[...]


def unfold_matrix(blocks, pieces, held):
    shape = (blocks * held, pieces * blocks * FOLD)
    row, column = iota(shape, 0), iota(shape, 1)
    slot = row % held
    source = (slot // FOLD) * (blocks * FOLD) + (row // held) * FOLD + slot % FOLD
    return jnp.where(jnp.logical_and(source == column, slot < pieces * FOLD), 1.0, 0.0).astype(BF16)


def raw_kernel(pieces, width, held, which_ref, in_ref, down_ref, *refs):
    out_ref = refs[-1]
    blocks = out_ref.shape[0]
    units = down_ref.shape[2]
    slots = pieces * FOLD
    folded = in_ref[:, 1 - which_ref[0]].astype(F32).reshape(blocks * FOLD, in_ref.shape[3])
    base = pieces * width
    spare = jnp.zeros((blocks * FOLD, 2 * LANES - width - 1), F32)
    stacked = []
    for piece in range(pieces):
        columns = [
            folded[:, piece * width : (piece + 1) * width],
            folded[:, base + piece : base + piece + 1],
            spare,
        ]
        stacked.append(jnp.concatenate(columns, axis=1))
    stacked = jnp.concatenate(stacked, axis=0).astype(BF16)
    rows = nn(unfold_matrix(blocks, pieces, held), stacked)
    arrived = rows[:, :width]
    first = rows[:, width : width + 1] == 0.0
    zero = jnp.zeros_like(arrived)
    raw = nn(jnp.where(first, arrived, zero).astype(BF16), down_ref[0])
    raw = raw + nn(jnp.where(first, zero, arrived).astype(BF16), down_ref[1])
    parts = pack(raw.reshape(blocks, held, units), slots)
    rows = parts[0].shape[1]
    for at, part in enumerate(parts):
        span = slice(at * rows, (at + 1) * rows)
        for to, chip in enumerate(chip_order(blocks)):
            block = part[blocks - 1 - chip]
            if len(refs) > 1:
                block = block + refs[0][to, span]
            out_ref[to, span] = block.astype(out_ref.dtype)


def lanes_of(column):
    shape = (column.shape[0], LANES)
    return jnp.sum(jnp.where(iota(shape, 0) == iota(shape, 1), column, 0.0), axis=0, keepdims=True)


def hidden_kernel(pieces, width, at_ref, parts_ref, in_ref, gate_ref, up_ref, out_ref):
    blocks, packed, _ = parts_ref.shape
    total = parts_ref[0].astype(F32)
    for at in range(1, blocks):
        total = total + parts_ref[at].astype(F32)
    slots, units = gate_ref.shape
    raw = jnp.concatenate(
        [total[tile * slots : (tile + 1) * slots] for tile in range(units // LANES)], axis=1
    )
    at = 2 * in_ref.shape[0] - 1 - at_ref[0]
    own = in_ref[at >> 1, at & 1].astype(F32)
    base = pieces * width
    picked = jnp.concatenate(
        [own[:, base + at : base + at + 1] for at in range(pieces)], axis=0
    )
    base = base + pieces
    weight = jnp.concatenate(
        [own[:, base + at : base + at + 1] for at in range(pieces)], axis=0
    )
    gate = gate_ref[...].astype(F32)
    up = up_ref[...].astype(F32)
    sig = jax.nn.sigmoid(gate)
    active = gate * sig
    router = jnp.sum(active * up * raw, axis=1, keepdims=True)
    scaled = weight * raw
    by_gate = scaled * up * sig * (1.0 + gate * (1.0 - sig))
    by_up = scaled * active
    spare = out_ref.shape[1] - 2 * packed
    row = iota((spare, LANES), 0)
    extra = jnp.where(row == 0, lanes_of(router), jnp.where(row == 1, lanes_of(picked), 0.0))
    block = jnp.concatenate(pack(by_gate, slots) + pack(by_up, slots) + [extra], axis=0)
    block = block.astype(BF16)
    for at in range(blocks):
        out_ref[at] = block


def back_kernel(pieces, width, held, merges, which_ref, in_ref, gate_ref, up_ref, *refs):
    out_ref = refs[-1]
    blocks = in_ref.shape[0]
    units = gate_ref.shape[2]
    tiles = units // LANES
    slots = pieces * FOLD
    packed = tiles * slots
    unfold = unfold_matrix(blocks, pieces, held)
    block = in_ref[...].astype(F32)

    def spread(start):
        parts = [
            block[:, start + tile * slots : start + tile * slots + held].reshape(
                blocks * held, LANES
            )
            for tile in range(tiles)
        ]
        return jnp.concatenate(parts, axis=1).astype(BF16)

    by_gate = spread(0)
    by_up = spread(packed)
    shape = (blocks, held, LANES)
    picked = jnp.where(
        iota(shape, 1) == iota(shape, 2), block[:, 2 * packed + 1 : 2 * packed + 2], 0.0
    )
    picked = jnp.sum(picked, axis=2, keepdims=True).reshape(blocks * held, 1)
    back = jnp.where(
        picked == 0.0,
        nt(by_gate, gate_ref[0]) + nt(by_up, up_ref[0]),
        nt(by_gate, gate_ref[1]) + nt(by_up, up_ref[1]),
    )
    folded = tn(unfold, back.astype(BF16))
    rows = blocks * FOLD
    parts = [folded[piece * rows : (piece + 1) * rows] for piece in range(pieces)]
    router = block[:, 2 * packed].astype(BF16)
    repeat = (iota((rows, blocks), 0) // FOLD == iota((rows, blocks), 1)).astype(F32).astype(BF16)
    router = nn(repeat, router)
    kept = jnp.logical_and(
        iota((rows, LANES), 1) % FOLD == iota((rows, LANES), 0) % FOLD,
        iota((rows, LANES), 1) < slots,
    )
    router = jnp.where(kept, router, 0.0).astype(BF16)
    lanes_left = out_ref.shape[-1] - pieces * width
    gather = iota((LANES, lanes_left), 0) // FOLD == iota((LANES, lanes_left), 1)
    parts.append(nn(router, gather.astype(F32).astype(BF16)))
    sent = jnp.concatenate(parts, axis=1)
    sent = sent.reshape(blocks, FOLD, sent.shape[1]).astype(BF16)
    if merges:
        which = which_ref[0]
        out_ref[:, 1 - which] = refs[0][...]
    for at, chip in enumerate(chip_order(blocks)):
        if merges:
            out_ref[chip, which] = sent[at]
        else:
            out_ref[chip] = sent[at]


def finish_kernel(pieces, width, in_ref, pick_ref, grad_ref, router_ref):
    nodes = in_ref.shape[0]
    pick = pick_ref[...]
    groups, tokens = pick.shape
    named, slot, hits = pair_maps(pick, nodes, False)
    rows = in_ref[...].astype(F32).reshape(nodes * FOLD, in_ref.shape[2])
    base = pieces * width
    total = jnp.zeros((width, tokens), F32)
    routed = jnp.zeros((nodes * FOLD, tokens), F32)
    for piece in range(pieces):
        place = placing(named, slot, piece)
        total = total + tn(
            rows[:, piece * width : (piece + 1) * width].astype(BF16), place.astype(BF16)
        )
        routed = routed + place * rows[:, base + piece : base + piece + 1]
    grad_ref[...] = total.astype(BF16)
    router = [jnp.sum(routed * hit, axis=0, keepdims=True) for hit in hits]
    router_ref[...] = jnp.concatenate(router, axis=0).astype(BF16)


def per_device(
    out_grad,
    node_pick,
    expert_pick,
    pick_weight,
    gate_weight,
    up_weight,
    down_weight,
    saved_gate,
    saved_up,
):
    nodes = lax.axis_size("node")
    local_count = lax.axis_size("local")
    tokens, width = out_grad.shape
    groups = node_pick.shape[1]
    experts, units = gate_weight.shape[1], gate_weight.shape[3]
    slots = saved_gate.shape[1]
    chips = local_count // 2
    pieces = slots // FOLD
    tiles = units // LANES
    half = nodes // 2
    held = round_up(slots, 8)
    packed = tiles * slots
    block = round_up(pieces * width + 2 * pieces, LANES)
    place = lax.axis_index("local").astype(jnp.int32)
    own = place.reshape(1)
    mine = own & 1
    other = 1 - mine
    same_core = [[2 * chip + c for chip in chip_order(chips)] for c in range(2)]
    backwards = [list(range(nodes))[::-1]]
    swap = [(at, at ^ 1) for at in range(local_count)]

    pick = node_pick.T
    gate_saved = saved_gate.reshape(slots, units)
    up_saved = saved_up.reshape(slots, units)
    down = jnp.swapaxes(down_weight[0], 1, 2)
    hbm = pl.BlockSpec(memory_space=pltpu.HBM)
    vmem = pl.BlockSpec(memory_space=pltpu.VMEM)
    smem = pl.BlockSpec(memory_space=pltpu.SMEM)

    sent = call(
        functools.partial(prepare_kernel, pieces),
        jax.ShapeDtypeStruct((nodes, FOLD, block), BF16),
        limit=VMEM_MOST,
        in_specs=[hbm] * 4,
        out_specs=vmem,
        scratch_shapes=[
            pltpu.VMEM((groups, tokens), jnp.int32),
            pltpu.VMEM((groups, 1, tokens), jnp.int32),
            pltpu.VMEM((groups, tokens), BF16),
            pltpu.VMEM((width, tokens), BF16),
            pltpu.SemaphoreType.DMA((4,)),
        ],
    )(pick, jnp.transpose(expert_pick, (1, 2, 0)), pick_weight[:, :, 0].T, out_grad.T)
    down = call(
        keep_kernel,
        jax.ShapeDtypeStruct(down.shape, BF16),
        in_specs=[vmem, hbm],
        out_specs=vmem,
    )(down, sent)
    other_down = lax.ppermute(down, "local", swap)
    arrived = lax.all_to_all(
        sent, "node", split_axis=0, concat_axis=0, axis_index_groups=backwards, tiled=True
    )
    arrived = arrived.reshape(half, 2, FOLD, block)

    def raw_part(rows, weight, dtype, *before):
        return call(
            functools.partial(raw_kernel, pieces, width, held),
            jax.ShapeDtypeStruct((half, packed, LANES), dtype),
            in_specs=[smem, vmem, vmem] + [vmem] * len(before),
            out_specs=vmem,
        )(mine, rows, weight, *before)

    received = lax.ppermute(arrived, "local", swap)
    partial = raw_part(arrived, down, F32)
    partial = raw_part(received, other_down, BF16, partial)
    parts = lax.all_to_all(
        partial, "local", split_axis=0, concat_axis=0, axis_index_groups=same_core, tiled=True
    )
    hidden = call(
        functools.partial(hidden_kernel, pieces, width),
        jax.ShapeDtypeStruct((chips, 2 * packed + 16, LANES), BF16),
        in_specs=[smem, vmem, vmem, vmem, vmem],
        out_specs=vmem,
    )(own, parts, arrived, gate_saved, up_saved)
    hidden_mine = lax.all_to_all(
        hidden, "local", split_axis=0, concat_axis=0, axis_index_groups=same_core, tiled=True
    )
    hidden_other = lax.ppermute(hidden_mine, "local", swap)
    back = call(
        functools.partial(back_kernel, pieces, width, held, False),
        jax.ShapeDtypeStruct((half, FOLD, block), BF16),
        in_specs=[smem, vmem, vmem, vmem],
        out_specs=vmem,
    )(mine, hidden_mine, gate_weight[0], up_weight[0])
    back = call(
        functools.partial(back_kernel, pieces, width, held, True),
        jax.ShapeDtypeStruct((half, 2, FOLD, block), BF16),
        in_specs=[smem, vmem, vmem, vmem, vmem],
        out_specs=vmem,
    )(other, hidden_other, gate_weight[0], up_weight[0], back)
    back = back.reshape(nodes, FOLD, block)
    returned = lax.all_to_all(back, "node", split_axis=0, concat_axis=0, tiled=True)
    grad, router = call(
        functools.partial(finish_kernel, pieces, width),
        (
            jax.ShapeDtypeStruct((width, tokens), BF16),
            jax.ShapeDtypeStruct((groups, tokens), BF16),
        ),
    )(returned, pick)
    return grad.T, router.T.reshape(tokens, groups, 1)


def solution(mesh):
    return jax.shard_map(
        per_device,
        mesh=mesh,
        in_specs=(
            P("node", "local"),
            P("node", None),
            P("node", None, None),
            P("node", None, None),
            P("node", None, "local", None),
            P("node", None, "local", None),
            P("node", None, None, "local"),
            P("node", "local", None, None),
            P("node", "local", None, None),
        ),
        out_specs=(P("node", "local"), P("node", None, None)),
        check_vma=False,
    )
```

```python
import functools

import jax
import jax.numpy as jnp
from jax import lax
from jax.experimental import pallas as pl
from jax.experimental.pallas import tpu as pltpu
from jax.sharding import PartitionSpec as P

BF16 = jnp.bfloat16
F32 = jnp.float32
LANES = 128
FOLD = 4
VMEM_LIMIT = 32 * 1024 * 1024
CURVE = (0, 1, 5, 4, 8, 12, 13, 9, 10, 14, 15, 11, 7, 6, 2, 3)
VMEM_MOST = 58 * 1024 * 1024


def round_up(value, unit):
    return -(-value // unit) * unit


def nn(a, b):
    return lax.dot_general(a, b, (((1,), (0,)), ((), ())), preferred_element_type=F32)


def nt(a, b):
    return lax.dot_general(a, b, (((1,), (1,)), ((), ())), preferred_element_type=F32)


def tn(a, b):
    return lax.dot_general(a, b, (((0,), (0,)), ((), ())), preferred_element_type=F32)


def iota(shape, axis):
    return lax.broadcasted_iota(jnp.int32, shape, axis)


def call(kernel, out_shape, limit=VMEM_LIMIT, **extra):
    return pl.pallas_call(
        kernel,
        out_shape=out_shape,
        compiler_params=pltpu.CompilerParams(vmem_limit_bytes=limit),
        **extra,
    )


def chip_order(chips):
    return CURVE if chips == len(CURVE) else tuple(range(chips))


def pair_maps(pick, nodes, backwards):
    groups, tokens = pick.shape
    rows = nodes * FOLD
    row = iota((rows, tokens), 0)
    node_of = row // FOLD
    if backwards:
        node_of = nodes - 1 - node_of
    hits = [pick[g : g + 1, :] == node_of for g in range(groups)]
    named = functools.reduce(jnp.logical_or, hits)
    earlier = (iota((tokens, tokens), 0) < iota((tokens, tokens), 1)).astype(F32).astype(BF16)
    slot = nn(named.astype(F32).astype(BF16), earlier).astype(jnp.int32)
    return jnp.where(named, slot - row % FOLD, -FOLD), hits


def placing(slot, piece):
    return jnp.where(slot == piece * FOLD, 1.0, 0.0)


def fetch(copies):
    for copy in copies:
        copy.start()


def pack(rows, slots):
    tiles = rows.shape[-1] // LANES
    axis = rows.ndim - 2
    pieces = [
        rows[..., :slots, tile * LANES : (tile + 1) * LANES] for tile in range(tiles)
    ]
    return [jnp.concatenate(pieces[at : at + 4], axis=axis) for at in range(0, tiles, 4)]


def prepare_kernel(
    pieces,
    pick_hbm,
    expert_hbm,
    weight_hbm,
    rows_hbm,
    out_ref,
    pick_ref,
    expert_ref,
    weight_ref,
    rows_ref,
    sems,
):
    pairs = [
        (pick_hbm, pick_ref),
        (expert_hbm, expert_ref),
        (weight_hbm, weight_ref),
        (rows_hbm, rows_ref),
    ]
    copies = [
        pltpu.make_async_copy(source, target, sems.at[at])
        for at, (source, target) in enumerate(pairs)
    ]
    fetch(copies)
    nodes = out_ref.shape[0]
    width, tokens = rows_ref.shape
    rows = nodes * FOLD
    for copy in copies:
        copy.wait()
    slot, hits = pair_maps(pick_ref[...], nodes, True)
    weights = weight_ref[...].astype(F32)
    signed = functools.reduce(
        jnp.add,
        [
            jnp.where(hit, weights[g : g + 1, :] * (1.0 - 2.0 * expert_ref[g].astype(F32)), 0.0)
            for g, hit in enumerate(hits)
        ],
    )
    spare = out_ref.shape[2] - pieces * width
    lane = iota((rows, spare), 1)
    meta = jnp.zeros((rows, spare), F32)
    places = [placing(slot, piece) for piece in range(pieces)]
    sent = nt(jnp.concatenate(places, axis=0).astype(BF16), rows_ref[...])
    for piece, place in enumerate(places):
        scale = jnp.sum(place * signed, axis=1, keepdims=True)
        meta = jnp.where(lane == piece, jnp.where(scale < 0.0, 1.0, 0.0), meta)
        meta = jnp.where(lane == pieces + piece, jnp.abs(scale), meta)
    parts = [sent[piece * rows : (piece + 1) * rows] for piece in range(pieces)]
    block = jnp.concatenate(parts + [meta], axis=1)
    out_ref[...] = block.reshape(nodes, FOLD, block.shape[1]).astype(BF16)


def keep_kernel(after_ref, *refs):
    half = len(refs) // 2
    for in_ref, out_ref in zip(refs[:half], refs[half:]):
        out_ref[...] = in_ref[...]


def unfold_matrix(blocks, pieces, held):
    shape = (blocks * held, pieces * blocks * FOLD)
    row, column = iota(shape, 0), iota(shape, 1)
    slot = row % held
    source = (slot // FOLD) * (blocks * FOLD) + (row // held) * FOLD + slot % FOLD
    return jnp.where(jnp.logical_and(source == column, slot < pieces * FOLD), 1.0, 0.0).astype(BF16)


def raw_kernel(pieces, width, held, which_ref, in_ref, down_ref, *refs):
    out_ref = refs[-1]
    blocks = out_ref.shape[0]
    units = down_ref.shape[2]
    slots = pieces * FOLD
    folded = in_ref[:, 1 - which_ref[0]].astype(F32).reshape(blocks * FOLD, in_ref.shape[3])
    base = pieces * width
    spare = jnp.zeros((blocks * FOLD, 2 * LANES - width - 1), F32)
    stacked = []
    for piece in range(pieces):
        columns = [
            folded[:, piece * width : (piece + 1) * width],
            folded[:, base + piece : base + piece + 1],
            spare,
        ]
        stacked.append(jnp.concatenate(columns, axis=1))
    stacked = jnp.concatenate(stacked, axis=0).astype(BF16)
    rows = nn(unfold_matrix(blocks, pieces, held), stacked)
    arrived = rows[:, :width]
    first = rows[:, width : width + 1] == 0.0
    zero = jnp.zeros_like(arrived)
    raw = nn(jnp.where(first, arrived, zero).astype(BF16), down_ref[0])
    raw = raw + nn(jnp.where(first, zero, arrived).astype(BF16), down_ref[1])
    parts = pack(raw.reshape(blocks, held, units), slots)
    rows = parts[0].shape[1]
    for at, part in enumerate(parts):
        span = slice(at * rows, (at + 1) * rows)
        for to, chip in enumerate(chip_order(blocks)):
            block = part[blocks - 1 - chip]
            if len(refs) > 1:
                block = block + refs[0][to, span]
            out_ref[to, span] = block.astype(out_ref.dtype)


def lanes_of(column):
    shape = (column.shape[0], LANES)
    return jnp.sum(jnp.where(iota(shape, 0) == iota(shape, 1), column, 0.0), axis=0, keepdims=True)


def hidden_kernel(pieces, width, at_ref, parts_ref, in_ref, gate_ref, up_ref, out_ref):
    blocks, packed, _ = parts_ref.shape
    total = parts_ref[0].astype(F32)
    for at in range(1, blocks):
        total = total + parts_ref[at].astype(F32)
    slots, units = gate_ref.shape
    raw = jnp.concatenate(
        [total[tile * slots : (tile + 1) * slots] for tile in range(units // LANES)], axis=1
    )
    at = 2 * in_ref.shape[0] - 1 - at_ref[0]
    own = in_ref[at >> 1, at & 1].astype(F32)
    base = pieces * width
    picked = jnp.concatenate(
        [own[:, base + at : base + at + 1] for at in range(pieces)], axis=0
    )
    base = base + pieces
    weight = jnp.concatenate(
        [own[:, base + at : base + at + 1] for at in range(pieces)], axis=0
    )
    gate = gate_ref[...].astype(F32)
    up = up_ref[...].astype(F32)
    sig = jax.nn.sigmoid(gate)
    active = gate * sig
    router = jnp.sum(active * up * raw, axis=1, keepdims=True)
    scaled = weight * raw
    by_gate = scaled * up * sig * (1.0 + gate * (1.0 - sig))
    by_up = scaled * active
    spare = out_ref.shape[1] - 2 * packed
    row = iota((spare, LANES), 0)
    extra = jnp.where(row == 0, lanes_of(router), jnp.where(row == 1, lanes_of(picked), 0.0))
    block = jnp.concatenate(pack(by_gate, slots) + pack(by_up, slots) + [extra], axis=0)
    block = block.astype(BF16)
    for at in range(blocks):
        out_ref[at] = block


def back_kernel(pieces, width, held, in_ref, gate_ref, up_ref, out_ref):
    blocks = in_ref.shape[0]
    units = gate_ref.shape[2]
    tiles = units // LANES
    slots = pieces * FOLD
    packed = tiles * slots
    unfold = unfold_matrix(blocks, pieces, held)
    block = in_ref[...].astype(F32)

    def spread(start):
        parts = [
            block[:, start + tile * slots : start + tile * slots + held].reshape(
                blocks * held, LANES
            )
            for tile in range(tiles)
        ]
        return jnp.concatenate(parts, axis=1).astype(BF16)

    by_gate = spread(0)
    by_up = spread(packed)
    shape = (blocks, held, LANES)
    picked = jnp.where(
        iota(shape, 1) == iota(shape, 2), block[:, 2 * packed + 1 : 2 * packed + 2], 0.0
    )
    picked = jnp.sum(picked, axis=2, keepdims=True).reshape(blocks * held, 1)
    back = jnp.where(
        picked == 0.0,
        nt(by_gate, gate_ref[0]) + nt(by_up, up_ref[0]),
        nt(by_gate, gate_ref[1]) + nt(by_up, up_ref[1]),
    )
    folded = tn(unfold, back.astype(BF16))
    rows = blocks * FOLD
    parts = [folded[piece * rows : (piece + 1) * rows] for piece in range(pieces)]
    router = block[:, 2 * packed].astype(BF16)
    repeat = (iota((rows, blocks), 0) // FOLD == iota((rows, blocks), 1)).astype(F32).astype(BF16)
    router = nn(repeat, router)
    kept = jnp.logical_and(
        iota((rows, LANES), 1) % FOLD == iota((rows, LANES), 0) % FOLD,
        iota((rows, LANES), 1) < slots,
    )
    router = jnp.where(kept, router, 0.0).astype(BF16)
    lanes_left = out_ref.shape[-1] - pieces * width
    gather = iota((LANES, lanes_left), 0) // FOLD == iota((LANES, lanes_left), 1)
    parts.append(nn(router, gather.astype(F32).astype(BF16)))
    sent = jnp.concatenate(parts, axis=1)
    sent = sent.reshape(blocks, FOLD, sent.shape[1]).astype(BF16)
    for at, chip in enumerate(chip_order(blocks)):
        out_ref[chip] = sent[at]


def merge_kernel(which_ref, mine_ref, other_ref, out_ref):
    which = which_ref[0]
    out_ref[:, which] = mine_ref[...]
    out_ref[:, 1 - which] = other_ref[...]


def finish_kernel(pieces, width, in_ref, pick_ref, grad_ref, router_ref):
    nodes = in_ref.shape[0]
    slot, hits = pair_maps(pick_ref[...], nodes, False)
    rows = in_ref[...].astype(F32).reshape(nodes * FOLD, in_ref.shape[2])
    base = pieces * width
    routed = jnp.zeros(slot.shape, F32)
    places = [placing(slot, piece) for piece in range(pieces)]
    for piece, place in enumerate(places):
        routed = routed + place * rows[:, base + piece : base + piece + 1]
    stacked = jnp.concatenate(
        [rows[:, piece * width : (piece + 1) * width] for piece in range(pieces)], axis=0
    )
    total = tn(stacked.astype(BF16), jnp.concatenate(places, axis=0).astype(BF16))
    grad_ref[...] = total.astype(BF16)
    router = [jnp.sum(jnp.where(hit, routed, 0.0), axis=0, keepdims=True) for hit in hits]
    router_ref[...] = jnp.concatenate(router, axis=0).astype(BF16)


def per_device(
    out_grad,
    node_pick,
    expert_pick,
    pick_weight,
    gate_weight,
    up_weight,
    down_weight,
    saved_gate,
    saved_up,
):
    nodes = lax.axis_size("node")
    local_count = lax.axis_size("local")
    tokens, width = out_grad.shape
    groups = node_pick.shape[1]
    experts, units = gate_weight.shape[1], gate_weight.shape[3]
    slots = saved_gate.shape[1]
    chips = local_count // 2
    pieces = slots // FOLD
    tiles = units // LANES
    half = nodes // 2
    held = round_up(slots, 8)
    packed = tiles * slots
    block = round_up(pieces * width + 2 * pieces, LANES)
    place = lax.axis_index("local").astype(jnp.int32)
    own = place.reshape(1)
    mine = own & 1
    same_core = [[2 * chip + c for chip in chip_order(chips)] for c in range(2)]
    backwards = [list(range(nodes))[::-1]]
    swap = [(at, at ^ 1) for at in range(local_count)]

    pick = node_pick.T
    gate_saved = saved_gate.reshape(slots, units)
    up_saved = saved_up.reshape(slots, units)
    down = jnp.swapaxes(down_weight[0], 1, 2)
    hbm = pl.BlockSpec(memory_space=pltpu.HBM)
    vmem = pl.BlockSpec(memory_space=pltpu.VMEM)
    smem = pl.BlockSpec(memory_space=pltpu.SMEM)

    sent = call(
        functools.partial(prepare_kernel, pieces),
        jax.ShapeDtypeStruct((nodes, FOLD, block), BF16),
        limit=VMEM_MOST,
        in_specs=[hbm] * 4,
        out_specs=vmem,
        scratch_shapes=[
            pltpu.VMEM((groups, tokens), jnp.int32),
            pltpu.VMEM((groups, 1, tokens), jnp.int32),
            pltpu.VMEM((groups, tokens), BF16),
            pltpu.VMEM((width, tokens), BF16),
            pltpu.SemaphoreType.DMA((4,)),
        ],
    )(pick, jnp.transpose(expert_pick, (1, 2, 0)), pick_weight[:, :, 0].T, out_grad.T)
    others = [lax.ppermute(weight[0], "local", swap) for weight in (gate_weight, up_weight)]

    def keep(after, limit, *weights):
        return call(
            keep_kernel,
            tuple(jax.ShapeDtypeStruct(weight.shape, BF16) for weight in weights),
            limit=limit,
            in_specs=[hbm] + [vmem] * len(weights),
            out_specs=(vmem,) * len(weights),
        )(after, *weights)

    others = keep(sent, VMEM_MOST, *others)
    (sent_down,) = keep(others[0], VMEM_LIMIT, down)
    other_down = lax.ppermute(sent_down, "local", swap)
    arrived = lax.all_to_all(
        sent, "node", split_axis=0, concat_axis=0, axis_index_groups=backwards, tiled=True
    )
    arrived = arrived.reshape(half, 2, FOLD, block)

    def raw_part(rows, weight, dtype, *before):
        return call(
            functools.partial(raw_kernel, pieces, width, held),
            jax.ShapeDtypeStruct((half, packed, LANES), dtype),
            in_specs=[smem, vmem, vmem] + [vmem] * len(before),
            out_specs=vmem,
        )(mine, rows, weight, *before)

    received = lax.ppermute(arrived, "local", swap)
    partial = raw_part(arrived, down, F32)
    partial = raw_part(received, other_down, BF16, partial)
    parts = lax.all_to_all(
        partial, "local", split_axis=0, concat_axis=0, axis_index_groups=same_core, tiled=True
    )
    hidden = call(
        functools.partial(hidden_kernel, pieces, width),
        jax.ShapeDtypeStruct((chips, 2 * packed + 16, LANES), BF16),
        in_specs=[smem, vmem, vmem, vmem, vmem],
        out_specs=vmem,
    )(own, parts, arrived, gate_saved, up_saved)
    hidden_mine = lax.all_to_all(
        hidden, "local", split_axis=0, concat_axis=0, axis_index_groups=same_core, tiled=True
    )

    def back_part(gate, up):
        return call(
            functools.partial(back_kernel, pieces, width, held),
            jax.ShapeDtypeStruct((half, FOLD, block), BF16),
            in_specs=[vmem] * 3,
            out_specs=vmem,
        )(hidden_mine, gate, up)

    theirs = lax.ppermute(back_part(*others), "local", swap)
    back = call(
        merge_kernel,
        jax.ShapeDtypeStruct((half, 2, FOLD, block), BF16),
        in_specs=[smem, vmem, vmem],
        out_specs=vmem,
    )(mine, back_part(gate_weight[0], up_weight[0]), theirs)
    back = back.reshape(nodes, FOLD, block)
    returned = lax.all_to_all(back, "node", split_axis=0, concat_axis=0, tiled=True)
    grad, router = call(
        functools.partial(finish_kernel, pieces, width),
        (
            jax.ShapeDtypeStruct((width, tokens), BF16),
            jax.ShapeDtypeStruct((groups, tokens), BF16),
        ),
    )(returned, pick)
    return grad.T, router.T.reshape(tokens, groups, 1)


def solution(mesh):
    return jax.shard_map(
        per_device,
        mesh=mesh,
        in_specs=(
            P("node", "local"),
            P("node", None),
            P("node", None, None),
            P("node", None, None),
            P("node", None, "local", None),
            P("node", None, "local", None),
            P("node", None, None, "local"),
            P("node", "local", None, None),
            P("node", "local", None, None),
        ),
        out_specs=(P("node", "local"), P("node", None, None)),
        check_vma=False,
    )
```

```python
import functools

import jax
import jax.numpy as jnp
from jax import lax
from jax.experimental import pallas as pl
from jax.experimental.pallas import tpu as pltpu
from jax.sharding import PartitionSpec as P

BF16 = jnp.bfloat16
F32 = jnp.float32
LANES = 128
FOLD = 4
VMEM_LIMIT = 32 * 1024 * 1024
VMEM_MOST = 58 * 1024 * 1024


def round_up(value, unit):
    return -(-value // unit) * unit


def nn(a, b):
    return lax.dot_general(a, b, (((1,), (0,)), ((), ())), preferred_element_type=F32)


def nt(a, b):
    return lax.dot_general(a, b, (((1,), (1,)), ((), ())), preferred_element_type=F32)


def tn(a, b):
    return lax.dot_general(a, b, (((0,), (0,)), ((), ())), preferred_element_type=F32)


def iota(shape, axis):
    return lax.broadcasted_iota(jnp.int32, shape, axis)


def call(kernel, out_shape, limit=VMEM_LIMIT, **extra):
    return pl.pallas_call(
        kernel,
        out_shape=out_shape,
        compiler_params=pltpu.CompilerParams(vmem_limit_bytes=limit),
        **extra,
    )


def pair_maps(pick, nodes):
    groups, tokens = pick.shape
    rows = nodes * FOLD
    row = iota((rows, tokens), 0)
    node_of = row // FOLD
    hits = [pick[g : g + 1, :] == node_of for g in range(groups)]
    named = functools.reduce(jnp.logical_or, hits)
    earlier = (iota((tokens, tokens), 0) < iota((tokens, tokens), 1)).astype(F32).astype(BF16)
    slot = nn(named.astype(F32).astype(BF16), earlier).astype(jnp.int32)
    return jnp.where(named, slot - row % FOLD, -FOLD), hits


def placing(slot, piece):
    return jnp.where(slot == piece * FOLD, 1.0, 0.0)


def fetch(copies):
    for copy in copies:
        copy.start()


def pack(rows, slots):
    tiles = rows.shape[-1] // LANES
    axis = rows.ndim - 2
    pieces = [
        rows[..., :slots, tile * LANES : (tile + 1) * LANES] for tile in range(tiles)
    ]
    return [jnp.concatenate(pieces[at : at + 4], axis=axis) for at in range(0, tiles, 4)]


def prepare_kernel(
    pieces,
    pick_hbm,
    expert_hbm,
    weight_hbm,
    rows_hbm,
    out_ref,
    pick_ref,
    expert_ref,
    weight_ref,
    rows_ref,
    sems,
):
    pairs = [
        (pick_hbm, pick_ref),
        (expert_hbm, expert_ref),
        (weight_hbm, weight_ref),
        (rows_hbm, rows_ref),
    ]
    copies = [
        pltpu.make_async_copy(source, target, sems.at[at])
        for at, (source, target) in enumerate(pairs)
    ]
    fetch(copies)
    nodes = out_ref.shape[0]
    width, tokens = rows_ref.shape
    rows = nodes * FOLD
    for copy in copies:
        copy.wait()
    slot, hits = pair_maps(pick_ref[...], nodes)
    weights = weight_ref[...].astype(F32)
    signed = functools.reduce(
        jnp.add,
        [
            jnp.where(hit, weights[g : g + 1, :] * (1.0 - 2.0 * expert_ref[g].astype(F32)), 0.0)
            for g, hit in enumerate(hits)
        ],
    )
    spare = out_ref.shape[2] - pieces * width
    lane = iota((rows, spare), 1)
    meta = jnp.zeros((rows, spare), F32)
    places = [placing(slot, piece) for piece in range(pieces)]
    sent = nt(jnp.concatenate(places, axis=0).astype(BF16), rows_ref[...])
    for piece, place in enumerate(places):
        scale = jnp.sum(place * signed, axis=1, keepdims=True)
        meta = jnp.where(lane == piece, jnp.where(scale < 0.0, 1.0, 0.0), meta)
        meta = jnp.where(lane == pieces + piece, jnp.abs(scale), meta)
    parts = [sent[piece * rows : (piece + 1) * rows] for piece in range(pieces)]
    block = jnp.concatenate(parts + [meta], axis=1)
    out_ref[...] = block.reshape(nodes, FOLD, block.shape[1]).astype(BF16)


def keep_kernel(after_ref, *refs):
    half = len(refs) // 2
    for in_ref, out_ref in zip(refs[:half], refs[half:]):
        out_ref[...] = in_ref[...]


def folded_row(row, blocks, pieces, held):
    block = row // held
    slot = row - block * held
    folded = (slot // FOLD) * (blocks * FOLD) + block * FOLD + slot % FOLD
    return jnp.where(slot < pieces * FOLD, folded, -1)


def unfold_matrix(blocks, pieces, held):
    rows, folds = blocks * held, pieces * blocks * FOLD
    source = folded_row(iota((rows, 1), 0), blocks, pieces, held)
    return jnp.where(iota((rows, folds), 1) == source, 1.0, 0.0).astype(BF16)


def fold_matrix(blocks, pieces, held):
    rows, folds = blocks * held, pieces * blocks * FOLD
    target = folded_row(iota((1, rows), 1), blocks, pieces, held)
    return jnp.where(iota((folds, rows), 0) == target, 1.0, 0.0).astype(BF16)


def raw_kernel(pieces, width, held, which_ref, in_ref, down_ref, *refs):
    out_ref = refs[-1]
    blocks = out_ref.shape[0]
    units = down_ref.shape[2]
    slots = pieces * FOLD
    folded = in_ref[:, which_ref[0]].astype(F32).reshape(blocks * FOLD, in_ref.shape[3])
    base = pieces * width
    spare = jnp.zeros((blocks * FOLD, 2 * LANES - width - 1), F32)
    stacked = []
    for piece in range(pieces):
        columns = [
            folded[:, piece * width : (piece + 1) * width],
            folded[:, base + piece : base + piece + 1],
            spare,
        ]
        stacked.append(jnp.concatenate(columns, axis=1))
    stacked = jnp.concatenate(stacked, axis=0).astype(BF16)
    rows = nn(unfold_matrix(blocks, pieces, held), stacked)
    arrived = rows[:, :width]
    first = rows[:, width : width + 1] == 0.0
    zero = jnp.zeros_like(arrived)
    raw = nn(jnp.where(first, arrived, zero).astype(BF16), down_ref[0])
    raw = raw + nn(jnp.where(first, zero, arrived).astype(BF16), down_ref[1])
    parts = pack(raw.reshape(blocks, held, units), slots)
    rows = parts[0].shape[1]
    for at, part in enumerate(parts):
        span = slice(at * rows, (at + 1) * rows)
        if len(refs) > 1:
            part = part + refs[0][:, span, :]
        out_ref[:, span, :] = part.astype(out_ref.dtype)


def lanes_of(column):
    shape = (column.shape[0], LANES)
    return jnp.sum(jnp.where(iota(shape, 0) == iota(shape, 1), column, 0.0), axis=0, keepdims=True)


def hidden_kernel(pieces, width, at_ref, parts_ref, in_ref, gate_ref, up_ref, out_ref):
    blocks, packed, _ = parts_ref.shape
    total = parts_ref[0].astype(F32)
    for at in range(1, blocks):
        total = total + parts_ref[at].astype(F32)
    slots, units = gate_ref.shape
    raw = jnp.concatenate(
        [total[tile * slots : (tile + 1) * slots] for tile in range(units // LANES)], axis=1
    )
    own = in_ref[at_ref[0] >> 1, at_ref[0] & 1].astype(F32)
    base = pieces * width
    picked = jnp.concatenate(
        [own[:, base + at : base + at + 1] for at in range(pieces)], axis=0
    )
    base = base + pieces
    weight = jnp.concatenate(
        [own[:, base + at : base + at + 1] for at in range(pieces)], axis=0
    )
    gate = gate_ref[...].astype(F32)
    up = up_ref[...].astype(F32)
    sig = jax.nn.sigmoid(gate)
    active = gate * sig
    router = jnp.sum(active * up * raw, axis=1, keepdims=True)
    scaled = weight * raw
    by_gate = scaled * up * sig * (1.0 + gate * (1.0 - sig))
    by_up = scaled * active
    spare = out_ref.shape[1] - 2 * packed
    row = iota((spare, LANES), 0)
    extra = jnp.where(row == 0, lanes_of(router), jnp.where(row == 1, lanes_of(picked), 0.0))
    block = jnp.concatenate(pack(by_gate, slots) + pack(by_up, slots) + [extra], axis=0)
    block = block.astype(BF16)
    for at in range(blocks):
        out_ref[at] = block


def back_kernel(pieces, width, held, in_ref, gate_ref, up_ref, out_ref):
    blocks = in_ref.shape[0]
    units = gate_ref.shape[2]
    tiles = units // LANES
    slots = pieces * FOLD
    packed = tiles * slots
    fold = fold_matrix(blocks, pieces, held)
    block = in_ref[...].astype(F32)

    def spread(start):
        parts = [
            block[:, start + tile * slots : start + tile * slots + held].reshape(
                blocks * held, LANES
            )
            for tile in range(tiles)
        ]
        return jnp.concatenate(parts, axis=1).astype(BF16)

    by_gate = spread(0)
    by_up = spread(packed)
    shape = (blocks, held, LANES)
    picked = jnp.where(
        iota(shape, 1) == iota(shape, 2), block[:, 2 * packed + 1 : 2 * packed + 2], 0.0
    )
    picked = jnp.sum(picked, axis=2, keepdims=True).reshape(blocks * held, 1)
    back = jnp.where(
        picked == 0.0,
        nt(by_gate, gate_ref[0]) + nt(by_up, up_ref[0]),
        nt(by_gate, gate_ref[1]) + nt(by_up, up_ref[1]),
    )
    folded = nn(fold, back.astype(BF16))
    rows = blocks * FOLD
    parts = [folded[piece * rows : (piece + 1) * rows] for piece in range(pieces)]
    router = block[:, 2 * packed].astype(BF16)
    repeat = (iota((rows, blocks), 0) // FOLD == iota((rows, blocks), 1)).astype(F32).astype(BF16)
    router = nn(repeat, router)
    kept = jnp.logical_and(
        iota((rows, LANES), 1) % FOLD == iota((rows, LANES), 0) % FOLD,
        iota((rows, LANES), 1) < slots,
    )
    router = jnp.where(kept, router, 0.0).astype(BF16)
    lanes_left = out_ref.shape[-1] - pieces * width
    gather = iota((LANES, lanes_left), 0) // FOLD == iota((LANES, lanes_left), 1)
    parts.append(nn(router, gather.astype(F32).astype(BF16)))
    sent = jnp.concatenate(parts, axis=1)
    sent = sent.reshape(blocks, FOLD, sent.shape[1]).astype(BF16)
    out_ref[...] = sent


def merge_kernel(which_ref, mine_ref, other_ref, out_ref):
    which = which_ref[0]
    out_ref[:, which] = mine_ref[...]
    out_ref[:, 1 - which] = other_ref[...]


def finish_kernel(pieces, width, in_ref, pick_ref, grad_ref, router_ref):
    nodes = in_ref.shape[0]
    slot, hits = pair_maps(pick_ref[...], nodes)
    rows = in_ref[...].astype(F32).reshape(nodes * FOLD, in_ref.shape[2])
    base = pieces * width
    routed = jnp.zeros(slot.shape, F32)
    places = [placing(slot, piece) for piece in range(pieces)]
    for piece, place in enumerate(places):
        routed = routed + place * rows[:, base + piece : base + piece + 1]
    stacked = jnp.concatenate(
        [rows[:, piece * width : (piece + 1) * width] for piece in range(pieces)], axis=0
    )
    total = tn(stacked.astype(BF16), jnp.concatenate(places, axis=0).astype(BF16))
    grad_ref[...] = total.astype(BF16)
    router = [jnp.sum(jnp.where(hit, routed, 0.0), axis=0, keepdims=True) for hit in hits]
    router_ref[...] = jnp.concatenate(router, axis=0).astype(BF16)


def per_device(
    out_grad,
    node_pick,
    expert_pick,
    pick_weight,
    gate_weight,
    up_weight,
    down_weight,
    saved_gate,
    saved_up,
):
    nodes = lax.axis_size("node")
    local_count = lax.axis_size("local")
    tokens, width = out_grad.shape
    groups = node_pick.shape[1]
    experts, units = gate_weight.shape[1], gate_weight.shape[3]
    slots = saved_gate.shape[1]
    chips = local_count // 2
    pieces = slots // FOLD
    tiles = units // LANES
    half = nodes // 2
    held = round_up(slots, 8)
    packed = tiles * slots
    block = round_up(pieces * width + 2 * pieces, LANES)
    place = lax.axis_index("local").astype(jnp.int32)
    own = place.reshape(1)
    mine = own & 1
    same_core = [[2 * chip + c for chip in range(chips)] for c in range(2)]
    swap = [(at, at ^ 1) for at in range(local_count)]

    pick = node_pick.T
    gate_saved = saved_gate.reshape(slots, units)
    up_saved = saved_up.reshape(slots, units)
    down = jnp.swapaxes(down_weight[0], 1, 2)
    hbm = pl.BlockSpec(memory_space=pltpu.HBM)
    vmem = pl.BlockSpec(memory_space=pltpu.VMEM)
    smem = pl.BlockSpec(memory_space=pltpu.SMEM)

    sent = call(
        functools.partial(prepare_kernel, pieces),
        jax.ShapeDtypeStruct((nodes, FOLD, block), BF16),
        limit=VMEM_MOST,
        in_specs=[hbm] * 4,
        out_specs=vmem,
        scratch_shapes=[
            pltpu.VMEM((groups, tokens), jnp.int32),
            pltpu.VMEM((groups, 1, tokens), jnp.int32),
            pltpu.VMEM((groups, tokens), BF16),
            pltpu.VMEM((width, tokens), BF16),
            pltpu.SemaphoreType.DMA((4,)),
        ],
    )(pick, jnp.transpose(expert_pick, (1, 2, 0)), pick_weight[:, :, 0].T, out_grad.T)
    others = [lax.ppermute(weight[0], "local", swap) for weight in (gate_weight, up_weight)]

    def keep(after, limit, *weights):
        return call(
            keep_kernel,
            tuple(jax.ShapeDtypeStruct(weight.shape, BF16) for weight in weights),
            limit=limit,
            in_specs=[hbm] + [vmem] * len(weights),
            out_specs=(vmem,) * len(weights),
        )(after, *weights)

    others = keep(sent, VMEM_MOST, *others)
    (sent_down,) = keep(others[0], VMEM_LIMIT, down)
    other_down = lax.ppermute(sent_down, "local", swap)
    arrived = lax.all_to_all(sent, "node", split_axis=0, concat_axis=0, tiled=True)
    arrived = arrived.reshape(half, 2, FOLD, block)

    def raw_part(rows, weight, dtype, *before):
        return call(
            functools.partial(raw_kernel, pieces, width, held),
            jax.ShapeDtypeStruct((half, packed, LANES), dtype),
            in_specs=[smem, vmem, vmem] + [vmem] * len(before),
            out_specs=vmem,
        )(mine, rows, weight, *before)

    received = lax.ppermute(arrived, "local", swap)
    partial = raw_part(arrived, down, F32)
    partial = raw_part(received, other_down, BF16, partial)
    parts = lax.all_to_all(
        partial, "local", split_axis=0, concat_axis=0, axis_index_groups=same_core, tiled=True
    )
    hidden = call(
        functools.partial(hidden_kernel, pieces, width),
        jax.ShapeDtypeStruct((chips, 2 * packed + 16, LANES), BF16),
        in_specs=[smem, vmem, vmem, vmem, vmem],
        out_specs=vmem,
    )(own, parts, arrived, gate_saved, up_saved)
    hidden_mine = lax.all_to_all(
        hidden, "local", split_axis=0, concat_axis=0, axis_index_groups=same_core, tiled=True
    )

    def back_part(gate, up):
        return call(
            functools.partial(back_kernel, pieces, width, held),
            jax.ShapeDtypeStruct((half, FOLD, block), BF16),
            in_specs=[vmem] * 3,
            out_specs=vmem,
        )(hidden_mine, gate, up)

    theirs = lax.ppermute(back_part(*others), "local", swap)
    back = call(
        merge_kernel,
        jax.ShapeDtypeStruct((half, 2, FOLD, block), BF16),
        in_specs=[smem, vmem, vmem],
        out_specs=vmem,
    )(mine, back_part(gate_weight[0], up_weight[0]), theirs)
    back = back.reshape(nodes, FOLD, block)
    returned = lax.all_to_all(back, "node", split_axis=0, concat_axis=0, tiled=True)
    grad, router = call(
        functools.partial(finish_kernel, pieces, width),
        (
            jax.ShapeDtypeStruct((width, tokens), BF16),
            jax.ShapeDtypeStruct((groups, tokens), BF16),
        ),
    )(returned, pick)
    return grad.T, router.T.reshape(tokens, groups, 1)


def solution(mesh):
    return jax.shard_map(
        per_device,
        mesh=mesh,
        in_specs=(
            P("node", "local"),
            P("node", None),
            P("node", None, None),
            P("node", None, None),
            P("node", None, "local", None),
            P("node", None, "local", None),
            P("node", None, None, "local"),
            P("node", "local", None, None),
            P("node", "local", None, None),
        ),
        out_specs=(P("node", "local"), P("node", None, None)),
        check_vma=False,
    )
```

```python
import functools

import jax
import jax.numpy as jnp
from jax import lax
from jax.experimental import pallas as pl
from jax.experimental.pallas import tpu as pltpu
from jax.sharding import PartitionSpec as P

BF16 = jnp.bfloat16
F32 = jnp.float32
LANES = 128
FOLD = 4
VMEM_LIMIT = 32 * 1024 * 1024
CURVE = (0, 1, 5, 4, 8, 12, 13, 9, 10, 14, 15, 11, 7, 6, 2, 3)
VMEM_MOST = 58 * 1024 * 1024


def round_up(value, unit):
    return -(-value // unit) * unit


def nn(a, b):
    return lax.dot_general(a, b, (((1,), (0,)), ((), ())), preferred_element_type=F32)


def nt(a, b):
    return lax.dot_general(a, b, (((1,), (1,)), ((), ())), preferred_element_type=F32)


def tn(a, b):
    return lax.dot_general(a, b, (((0,), (0,)), ((), ())), preferred_element_type=F32)


def iota(shape, axis):
    return lax.broadcasted_iota(jnp.int32, shape, axis)


def call(kernel, out_shape, limit=VMEM_LIMIT, **extra):
    return pl.pallas_call(
        kernel,
        out_shape=out_shape,
        compiler_params=pltpu.CompilerParams(vmem_limit_bytes=limit),
        **extra,
    )


def chip_order(chips):
    return CURVE if chips == len(CURVE) else tuple(range(chips))


def pair_maps(pick, nodes):
    groups, tokens = pick.shape
    rows = nodes * FOLD
    row = iota((rows, tokens), 0)
    node_of = nodes - 1 - row // FOLD
    hits = [pick[g : g + 1, :] == node_of for g in range(groups)]
    named = functools.reduce(jnp.logical_or, hits)
    earlier = (iota((tokens, tokens), 0) < iota((tokens, tokens), 1)).astype(F32).astype(BF16)
    slot = nn(named.astype(F32).astype(BF16), earlier).astype(jnp.int32)
    return jnp.where(named, slot - row % FOLD, -FOLD), hits


def placing(slot, piece):
    return jnp.where(slot == piece * FOLD, 1.0, 0.0)


def fetch(copies):
    for copy in copies:
        copy.start()


def pack(rows, slots):
    tiles = rows.shape[-1] // LANES
    axis = rows.ndim - 2
    pieces = [
        rows[..., :slots, tile * LANES : (tile + 1) * LANES] for tile in range(tiles)
    ]
    return [jnp.concatenate(pieces[at : at + 4], axis=axis) for at in range(0, tiles, 4)]


def prepare_kernel(
    pieces,
    pick_hbm,
    expert_hbm,
    weight_hbm,
    rows_hbm,
    out_ref,
    pick_ref,
    expert_ref,
    weight_ref,
    rows_ref,
    sems,
):
    pairs = [
        (pick_hbm, pick_ref),
        (expert_hbm, expert_ref),
        (weight_hbm, weight_ref),
        (rows_hbm, rows_ref),
    ]
    copies = [
        pltpu.make_async_copy(source, target, sems.at[at])
        for at, (source, target) in enumerate(pairs)
    ]
    fetch(copies)
    nodes = out_ref.shape[0]
    width, tokens = rows_ref.shape
    rows = nodes * FOLD
    for copy in copies:
        copy.wait()
    slot, hits = pair_maps(pick_ref[...], nodes)
    weights = weight_ref[...].astype(F32)
    signed = functools.reduce(
        jnp.add,
        [
            jnp.where(hit, weights[g : g + 1, :] * (1.0 - 2.0 * expert_ref[g].astype(F32)), 0.0)
            for g, hit in enumerate(hits)
        ],
    )
    spare = out_ref.shape[2] - pieces * width
    lane = iota((rows, spare), 1)
    meta = jnp.zeros((rows, spare), F32)
    places = [placing(slot, piece) for piece in range(pieces)]
    sent = nt(jnp.concatenate(places, axis=0).astype(BF16), rows_ref[...])
    for piece, place in enumerate(places):
        scale = jnp.sum(place * signed, axis=1, keepdims=True)
        meta = jnp.where(lane == piece, jnp.where(scale < 0.0, 1.0, 0.0), meta)
        meta = jnp.where(lane == pieces + piece, jnp.abs(scale), meta)
    parts = [sent[piece * rows : (piece + 1) * rows] for piece in range(pieces)]
    block = jnp.concatenate(parts + [meta], axis=1)
    out_ref[...] = block.reshape(nodes, FOLD, block.shape[1]).astype(BF16)


def keep_kernel(after_ref, *refs):
    half = len(refs) // 2
    for in_ref, out_ref in zip(refs[:half], refs[half:]):
        out_ref[...] = in_ref[...]


def folded_row(row, blocks, pieces, held):
    block = row // held
    slot = row - block * held
    folded = (slot // FOLD) * (blocks * FOLD) + block * FOLD + slot % FOLD
    return jnp.where(slot < pieces * FOLD, folded, -1)


def unfold_matrix(blocks, pieces, held):
    rows, folds = blocks * held, pieces * blocks * FOLD
    source = folded_row(iota((rows, 1), 0), blocks, pieces, held)
    return jnp.where(iota((rows, folds), 1) == source, 1.0, 0.0).astype(BF16)


def fold_matrix(blocks, pieces, held):
    rows, folds = blocks * held, pieces * blocks * FOLD
    target = folded_row(iota((1, rows), 1), blocks, pieces, held)
    return jnp.where(iota((folds, rows), 0) == target, 1.0, 0.0).astype(BF16)


def raw_kernel(pieces, width, held, which_ref, in_ref, down_ref, *refs):
    out_ref = refs[-1]
    blocks = out_ref.shape[0]
    units = down_ref.shape[2]
    slots = pieces * FOLD
    folded = in_ref[:, 1 - which_ref[0]].astype(F32).reshape(blocks * FOLD, in_ref.shape[3])
    base = pieces * width
    spare = jnp.zeros((blocks * FOLD, 2 * LANES - width - 1), F32)
    stacked = []
    for piece in range(pieces):
        columns = [
            folded[:, piece * width : (piece + 1) * width],
            folded[:, base + piece : base + piece + 1],
            spare,
        ]
        stacked.append(jnp.concatenate(columns, axis=1))
    stacked = jnp.concatenate(stacked, axis=0).astype(BF16)
    rows = nn(unfold_matrix(blocks, pieces, held), stacked)
    arrived = rows[:, :width]
    first = rows[:, width : width + 1] == 0.0
    zero = jnp.zeros_like(arrived)
    raw = nn(jnp.where(first, arrived, zero).astype(BF16), down_ref[0])
    raw = raw + nn(jnp.where(first, zero, arrived).astype(BF16), down_ref[1])
    parts = pack(raw.reshape(blocks, held, units), slots)
    rows = parts[0].shape[1]
    for at, part in enumerate(parts):
        span = slice(at * rows, (at + 1) * rows)
        for to, chip in enumerate(chip_order(blocks)):
            block = part[blocks - 1 - chip]
            if len(refs) > 1:
                block = block + refs[0][to, span]
            out_ref[to, span] = block.astype(out_ref.dtype)


def lanes_of(column):
    shape = (column.shape[0], LANES)
    return jnp.sum(jnp.where(iota(shape, 0) == iota(shape, 1), column, 0.0), axis=0, keepdims=True)


def hidden_kernel(pieces, width, at_ref, parts_ref, in_ref, gate_ref, up_ref, out_ref):
    blocks, packed, _ = parts_ref.shape
    total = parts_ref[0].astype(F32)
    for at in range(1, blocks):
        total = total + parts_ref[at].astype(F32)
    slots, units = gate_ref.shape
    raw = jnp.concatenate(
        [total[tile * slots : (tile + 1) * slots] for tile in range(units // LANES)], axis=1
    )
    at = 2 * in_ref.shape[0] - 1 - at_ref[0]
    own = in_ref[at >> 1, at & 1].astype(F32)
    base = pieces * width
    picked = jnp.concatenate(
        [own[:, base + at : base + at + 1] for at in range(pieces)], axis=0
    )
    base = base + pieces
    weight = jnp.concatenate(
        [own[:, base + at : base + at + 1] for at in range(pieces)], axis=0
    )
    gate = gate_ref[...].astype(F32)
    up = up_ref[...].astype(F32)
    sig = jax.nn.sigmoid(gate)
    active = gate * sig
    router = jnp.sum(active * up * raw, axis=1, keepdims=True)
    scaled = weight * raw
    by_gate = scaled * up * sig * (1.0 + gate * (1.0 - sig))
    by_up = scaled * active
    spare = out_ref.shape[1] - 2 * packed
    row = iota((spare, LANES), 0)
    extra = jnp.where(row == 0, lanes_of(router), jnp.where(row == 1, lanes_of(picked), 0.0))
    block = jnp.concatenate(pack(by_gate, slots) + pack(by_up, slots) + [extra], axis=0)
    block = block.astype(BF16)
    for at in range(blocks):
        out_ref[at] = block


def back_kernel(pieces, width, held, in_ref, gate_ref, up_ref, out_ref):
    blocks = in_ref.shape[0]
    units = gate_ref.shape[2]
    tiles = units // LANES
    slots = pieces * FOLD
    packed = tiles * slots
    fold = fold_matrix(blocks, pieces, held)
    block = in_ref[...].astype(F32)

    def spread(start):
        parts = [
            block[:, start + tile * slots : start + tile * slots + held].reshape(
                blocks * held, LANES
            )
            for tile in range(tiles)
        ]
        return jnp.concatenate(parts, axis=1).astype(BF16)

    by_gate = spread(0)
    by_up = spread(packed)
    shape = (blocks, held, LANES)
    picked = jnp.where(
        iota(shape, 1) == iota(shape, 2), block[:, 2 * packed + 1 : 2 * packed + 2], 0.0
    )
    picked = jnp.sum(picked, axis=2, keepdims=True).reshape(blocks * held, 1)
    back = jnp.where(
        picked == 0.0,
        nt(by_gate, gate_ref[0]) + nt(by_up, up_ref[0]),
        nt(by_gate, gate_ref[1]) + nt(by_up, up_ref[1]),
    )
    folded = nn(fold, back.astype(BF16))
    rows = blocks * FOLD
    parts = [folded[piece * rows : (piece + 1) * rows] for piece in range(pieces)]
    router = block[:, 2 * packed].astype(BF16)
    repeat = (iota((rows, blocks), 0) // FOLD == iota((rows, blocks), 1)).astype(F32).astype(BF16)
    router = nn(repeat, router)
    kept = jnp.logical_and(
        iota((rows, LANES), 1) % FOLD == iota((rows, LANES), 0) % FOLD,
        iota((rows, LANES), 1) < slots,
    )
    router = jnp.where(kept, router, 0.0).astype(BF16)
    lanes_left = out_ref.shape[-1] - pieces * width
    gather = iota((LANES, lanes_left), 0) // FOLD == iota((LANES, lanes_left), 1)
    parts.append(nn(router, gather.astype(F32).astype(BF16)))
    sent = jnp.concatenate(parts, axis=1)
    sent = sent.reshape(blocks, FOLD, sent.shape[1]).astype(BF16)
    for at, chip in enumerate(chip_order(blocks)):
        out_ref[blocks - 1 - chip] = sent[at]


def merge_kernel(which_ref, mine_ref, other_ref, out_ref):
    which = which_ref[0]
    out_ref[:, 1 - which] = mine_ref[...]
    out_ref[:, which] = other_ref[...]


def finish_kernel(pieces, width, in_ref, pick_ref, grad_ref, router_ref):
    nodes = in_ref.shape[0]
    slot, hits = pair_maps(pick_ref[...], nodes)
    rows = in_ref[...].astype(F32).reshape(nodes * FOLD, in_ref.shape[2])
    base = pieces * width
    routed = jnp.zeros(slot.shape, F32)
    places = [placing(slot, piece) for piece in range(pieces)]
    for piece, place in enumerate(places):
        routed = routed + place * rows[:, base + piece : base + piece + 1]
    stacked = jnp.concatenate(
        [rows[:, piece * width : (piece + 1) * width] for piece in range(pieces)], axis=0
    )
    total = tn(stacked.astype(BF16), jnp.concatenate(places, axis=0).astype(BF16))
    grad_ref[...] = total.astype(BF16)
    router = [jnp.sum(jnp.where(hit, routed, 0.0), axis=0, keepdims=True) for hit in hits]
    router_ref[...] = jnp.concatenate(router, axis=0).astype(BF16)


def per_device(
    out_grad,
    node_pick,
    expert_pick,
    pick_weight,
    gate_weight,
    up_weight,
    down_weight,
    saved_gate,
    saved_up,
):
    nodes = lax.axis_size("node")
    local_count = lax.axis_size("local")
    tokens, width = out_grad.shape
    groups = node_pick.shape[1]
    experts, units = gate_weight.shape[1], gate_weight.shape[3]
    slots = saved_gate.shape[1]
    chips = local_count // 2
    pieces = slots // FOLD
    tiles = units // LANES
    half = nodes // 2
    held = round_up(slots, 8)
    packed = tiles * slots
    block = round_up(pieces * width + 2 * pieces, LANES)
    place = lax.axis_index("local").astype(jnp.int32)
    own = place.reshape(1)
    mine = own & 1
    same_core = [[2 * chip + c for chip in chip_order(chips)] for c in range(2)]
    backwards = [list(range(nodes))[::-1]]
    swap = [(at, at ^ 1) for at in range(local_count)]

    pick = node_pick.T
    gate_saved = saved_gate.reshape(slots, units)
    up_saved = saved_up.reshape(slots, units)
    down = jnp.swapaxes(down_weight[0], 1, 2)
    hbm = pl.BlockSpec(memory_space=pltpu.HBM)
    vmem = pl.BlockSpec(memory_space=pltpu.VMEM)
    smem = pl.BlockSpec(memory_space=pltpu.SMEM)

    sent = call(
        functools.partial(prepare_kernel, pieces),
        jax.ShapeDtypeStruct((nodes, FOLD, block), BF16),
        limit=VMEM_MOST,
        in_specs=[hbm] * 4,
        out_specs=vmem,
        scratch_shapes=[
            pltpu.VMEM((groups, tokens), jnp.int32),
            pltpu.VMEM((groups, 1, tokens), jnp.int32),
            pltpu.VMEM((groups, tokens), BF16),
            pltpu.VMEM((width, tokens), BF16),
            pltpu.SemaphoreType.DMA((4,)),
        ],
    )(pick, jnp.transpose(expert_pick, (1, 2, 0)), pick_weight[:, :, 0].T, out_grad.T)
    others = [lax.ppermute(weight[0], "local", swap) for weight in (gate_weight, up_weight)]

    def keep(after, limit, *weights):
        return call(
            keep_kernel,
            tuple(jax.ShapeDtypeStruct(weight.shape, BF16) for weight in weights),
            limit=limit,
            in_specs=[hbm] + [vmem] * len(weights),
            out_specs=(vmem,) * len(weights),
        )(after, *weights)

    others = keep(sent, VMEM_MOST, *others)
    (sent_down,) = keep(others[0], VMEM_LIMIT, down)
    other_down = lax.ppermute(sent_down, "local", swap)
    arrived = lax.all_to_all(
        sent, "node", split_axis=0, concat_axis=0, axis_index_groups=backwards, tiled=True
    )
    arrived = arrived.reshape(half, 2, FOLD, block)

    def raw_part(rows, weight, dtype, *before):
        return call(
            functools.partial(raw_kernel, pieces, width, held),
            jax.ShapeDtypeStruct((half, packed, LANES), dtype),
            in_specs=[smem, vmem, vmem] + [vmem] * len(before),
            out_specs=vmem,
        )(mine, rows, weight, *before)

    received = lax.ppermute(arrived, "local", swap)
    partial = raw_part(arrived, down, F32)
    partial = raw_part(received, other_down, BF16, partial)
    parts = lax.all_to_all(
        partial, "local", split_axis=0, concat_axis=0, axis_index_groups=same_core, tiled=True
    )
    hidden = call(
        functools.partial(hidden_kernel, pieces, width),
        jax.ShapeDtypeStruct((chips, 2 * packed + 16, LANES), BF16),
        in_specs=[smem, vmem, vmem, vmem, vmem],
        out_specs=vmem,
    )(own, parts, arrived, gate_saved, up_saved)
    hidden_mine = lax.all_to_all(
        hidden, "local", split_axis=0, concat_axis=0, axis_index_groups=same_core, tiled=True
    )

    def back_part(gate, up):
        return call(
            functools.partial(back_kernel, pieces, width, held),
            jax.ShapeDtypeStruct((half, FOLD, block), BF16),
            in_specs=[vmem] * 3,
            out_specs=vmem,
        )(hidden_mine, gate, up)

    theirs = lax.ppermute(back_part(*others), "local", swap)
    back = call(
        merge_kernel,
        jax.ShapeDtypeStruct((half, 2, FOLD, block), BF16),
        in_specs=[smem, vmem, vmem],
        out_specs=vmem,
    )(mine, back_part(gate_weight[0], up_weight[0]), theirs)
    back = back.reshape(nodes, FOLD, block)
    returned = lax.all_to_all(
        back, "node", split_axis=0, concat_axis=0, axis_index_groups=backwards, tiled=True
    )
    grad, router = call(
        functools.partial(finish_kernel, pieces, width),
        (
            jax.ShapeDtypeStruct((width, tokens), BF16),
            jax.ShapeDtypeStruct((groups, tokens), BF16),
        ),
    )(returned, pick)
    return grad.T, router.T.reshape(tokens, groups, 1)


def solution(mesh):
    return jax.shard_map(
        per_device,
        mesh=mesh,
        in_specs=(
            P("node", "local"),
            P("node", None),
            P("node", None, None),
            P("node", None, None),
            P("node", None, "local", None),
            P("node", None, "local", None),
            P("node", None, None, "local"),
            P("node", "local", None, None),
            P("node", "local", None, None),
        ),
        out_specs=(P("node", "local"), P("node", None, None)),
        check_vma=False,
    )
```

```python
import functools

import jax
import jax.numpy as jnp
from jax import lax
from jax.experimental import pallas as pl
from jax.experimental.pallas import tpu as pltpu
from jax.sharding import PartitionSpec as P

BF16 = jnp.bfloat16
F32 = jnp.float32
LANES = 128
FOLD = 4
VMEM_LIMIT = 32 * 1024 * 1024
CURVE = (0, 1, 5, 4, 8, 12, 13, 9, 10, 14, 15, 11, 7, 6, 2, 3)
VMEM_MOST = 58 * 1024 * 1024


def round_up(value, unit):
    return -(-value // unit) * unit


def nn(a, b):
    return lax.dot_general(a, b, (((1,), (0,)), ((), ())), preferred_element_type=F32)


def nt(a, b):
    return lax.dot_general(a, b, (((1,), (1,)), ((), ())), preferred_element_type=F32)


def tn(a, b):
    return lax.dot_general(a, b, (((0,), (0,)), ((), ())), preferred_element_type=F32)


def iota(shape, axis):
    return lax.broadcasted_iota(jnp.int32, shape, axis)


def call(kernel, out_shape, limit=VMEM_LIMIT, **extra):
    return pl.pallas_call(
        kernel,
        out_shape=out_shape,
        compiler_params=pltpu.CompilerParams(vmem_limit_bytes=limit),
        **extra,
    )


def chip_order(chips):
    return CURVE if chips == len(CURVE) else tuple(range(chips))


def pair_maps(pick, nodes):
    groups, tokens = pick.shape
    rows = nodes * FOLD
    row = iota((rows, tokens), 0)
    node_of = (3 * nodes // 2 - 1 - row // FOLD) % nodes
    hits = [pick[g : g + 1, :] == node_of for g in range(groups)]
    named = functools.reduce(jnp.logical_or, hits)
    earlier = (iota((tokens, tokens), 0) < iota((tokens, tokens), 1)).astype(F32).astype(BF16)
    slot = nn(named.astype(F32).astype(BF16), earlier).astype(jnp.int32)
    return jnp.where(named, slot - row % FOLD, -FOLD), hits


def placing(slot, piece):
    return jnp.where(slot == piece * FOLD, 1.0, 0.0)


def fetch(copies):
    for copy in copies:
        copy.start()


def pack(rows, slots):
    tiles = rows.shape[-1] // LANES
    axis = rows.ndim - 2
    pieces = [
        rows[..., :slots, tile * LANES : (tile + 1) * LANES] for tile in range(tiles)
    ]
    return [jnp.concatenate(pieces[at : at + 4], axis=axis) for at in range(0, tiles, 4)]


def prepare_kernel(
    pieces,
    pick_hbm,
    expert_hbm,
    weight_hbm,
    rows_hbm,
    out_ref,
    pick_ref,
    expert_ref,
    weight_ref,
    rows_ref,
    sems,
):
    pairs = [
        (pick_hbm, pick_ref),
        (expert_hbm, expert_ref),
        (weight_hbm, weight_ref),
        (rows_hbm, rows_ref),
    ]
    copies = [
        pltpu.make_async_copy(source, target, sems.at[at])
        for at, (source, target) in enumerate(pairs)
    ]
    fetch(copies)
    nodes = out_ref.shape[0]
    width, tokens = rows_ref.shape
    rows = nodes * FOLD
    for copy in copies:
        copy.wait()
    slot, hits = pair_maps(pick_ref[...], nodes)
    weights = weight_ref[...].astype(F32)
    signed = functools.reduce(
        jnp.add,
        [
            jnp.where(hit, weights[g : g + 1, :] * (1.0 - 2.0 * expert_ref[g].astype(F32)), 0.0)
            for g, hit in enumerate(hits)
        ],
    )
    spare = out_ref.shape[2] - pieces * width
    lane = iota((rows, spare), 1)
    meta = jnp.zeros((rows, spare), F32)
    places = [placing(slot, piece) for piece in range(pieces)]
    sent = nt(jnp.concatenate(places, axis=0).astype(BF16), rows_ref[...])
    for piece, place in enumerate(places):
        scale = jnp.sum(place * signed, axis=1, keepdims=True)
        meta = jnp.where(lane == piece, jnp.where(scale < 0.0, 1.0, 0.0), meta)
        meta = jnp.where(lane == pieces + piece, jnp.abs(scale), meta)
    parts = [sent[piece * rows : (piece + 1) * rows] for piece in range(pieces)]
    block = jnp.concatenate(parts + [meta], axis=1)
    out_ref[...] = block.reshape(nodes, FOLD, block.shape[1]).astype(BF16)


def keep_kernel(after_ref, *refs):
    half = len(refs) // 2
    for in_ref, out_ref in zip(refs[:half], refs[half:]):
        out_ref[...] = in_ref[...]


def folded_row(row, blocks, pieces, held):
    block = row // held
    slot = row - block * held
    folded = (slot // FOLD) * (blocks * FOLD) + block * FOLD + slot % FOLD
    return jnp.where(slot < pieces * FOLD, folded, -1)


def unfold_matrix(blocks, pieces, held):
    rows, folds = blocks * held, pieces * blocks * FOLD
    source = folded_row(iota((rows, 1), 0), blocks, pieces, held)
    return jnp.where(iota((rows, folds), 1) == source, 1.0, 0.0).astype(BF16)


def fold_matrix(blocks, pieces, held):
    rows, folds = blocks * held, pieces * blocks * FOLD
    target = folded_row(iota((1, rows), 1), blocks, pieces, held)
    return jnp.where(iota((folds, rows), 0) == target, 1.0, 0.0).astype(BF16)


def raw_kernel(pieces, width, held, which_ref, in_ref, down_ref, *refs):
    out_ref = refs[-1]
    blocks = out_ref.shape[0]
    units = down_ref.shape[2]
    slots = pieces * FOLD
    folded = in_ref[:, 1 - which_ref[0]].astype(F32).reshape(blocks * FOLD, in_ref.shape[3])
    base = pieces * width
    spare = jnp.zeros((blocks * FOLD, 2 * LANES - width - 1), F32)
    stacked = []
    for piece in range(pieces):
        columns = [
            folded[:, piece * width : (piece + 1) * width],
            folded[:, base + piece : base + piece + 1],
            spare,
        ]
        stacked.append(jnp.concatenate(columns, axis=1))
    stacked = jnp.concatenate(stacked, axis=0).astype(BF16)
    rows = nn(unfold_matrix(blocks, pieces, held), stacked)
    arrived = rows[:, :width]
    first = rows[:, width : width + 1] == 0.0
    zero = jnp.zeros_like(arrived)
    raw = nn(jnp.where(first, arrived, zero).astype(BF16), down_ref[0])
    raw = raw + nn(jnp.where(first, zero, arrived).astype(BF16), down_ref[1])
    parts = pack(raw.reshape(blocks, held, units), slots)
    rows = parts[0].shape[1]
    for at, part in enumerate(parts):
        span = slice(at * rows, (at + 1) * rows)
        for to, chip in enumerate(chip_order(blocks)):
            block = part[(3 * blocks // 2 - 1 - chip) % blocks]
            if len(refs) > 1:
                block = block + refs[0][to, span]
            out_ref[to, span] = block.astype(out_ref.dtype)


def lanes_of(column):
    shape = (column.shape[0], LANES)
    return jnp.sum(jnp.where(iota(shape, 0) == iota(shape, 1), column, 0.0), axis=0, keepdims=True)


def hidden_kernel(pieces, width, at_ref, parts_ref, in_ref, gate_ref, up_ref, out_ref):
    blocks, packed, _ = parts_ref.shape
    total = parts_ref[0].astype(F32)
    for at in range(1, blocks):
        total = total + parts_ref[at].astype(F32)
    slots, units = gate_ref.shape
    raw = jnp.concatenate(
        [total[tile * slots : (tile + 1) * slots] for tile in range(units // LANES)], axis=1
    )
    at = (3 * in_ref.shape[0] - 1 - at_ref[0]) & (2 * in_ref.shape[0] - 1)
    own = in_ref[at >> 1, at & 1].astype(F32)
    base = pieces * width
    picked = jnp.concatenate(
        [own[:, base + at : base + at + 1] for at in range(pieces)], axis=0
    )
    base = base + pieces
    weight = jnp.concatenate(
        [own[:, base + at : base + at + 1] for at in range(pieces)], axis=0
    )
    gate = gate_ref[...].astype(F32)
    up = up_ref[...].astype(F32)
    sig = jax.nn.sigmoid(gate)
    active = gate * sig
    router = jnp.sum(active * up * raw, axis=1, keepdims=True)
    scaled = weight * raw
    by_gate = scaled * up * sig * (1.0 + gate * (1.0 - sig))
    by_up = scaled * active
    spare = out_ref.shape[1] - 2 * packed
    row = iota((spare, LANES), 0)
    extra = jnp.where(row == 0, lanes_of(router), jnp.where(row == 1, lanes_of(picked), 0.0))
    block = jnp.concatenate(pack(by_gate, slots) + pack(by_up, slots) + [extra], axis=0)
    block = block.astype(BF16)
    for at in range(blocks):
        out_ref[at] = block


def back_kernel(pieces, width, held, in_ref, gate_ref, up_ref, out_ref):
    blocks = in_ref.shape[0]
    units = gate_ref.shape[2]
    tiles = units // LANES
    slots = pieces * FOLD
    packed = tiles * slots
    fold = fold_matrix(blocks, pieces, held)
    block = in_ref[...].astype(F32)

    def spread(start):
        parts = [
            block[:, start + tile * slots : start + tile * slots + held].reshape(
                blocks * held, LANES
            )
            for tile in range(tiles)
        ]
        return jnp.concatenate(parts, axis=1).astype(BF16)

    by_gate = spread(0)
    by_up = spread(packed)
    shape = (blocks, held, LANES)
    picked = jnp.where(
        iota(shape, 1) == iota(shape, 2), block[:, 2 * packed + 1 : 2 * packed + 2], 0.0
    )
    picked = jnp.sum(picked, axis=2, keepdims=True).reshape(blocks * held, 1)
    back = jnp.where(
        picked == 0.0,
        nt(by_gate, gate_ref[0]) + nt(by_up, up_ref[0]),
        nt(by_gate, gate_ref[1]) + nt(by_up, up_ref[1]),
    )
    folded = nn(fold, back.astype(BF16))
    rows = blocks * FOLD
    parts = [folded[piece * rows : (piece + 1) * rows] for piece in range(pieces)]
    router = block[:, 2 * packed].astype(BF16)
    repeat = (iota((rows, blocks), 0) // FOLD == iota((rows, blocks), 1)).astype(F32).astype(BF16)
    router = nn(repeat, router)
    kept = jnp.logical_and(
        iota((rows, LANES), 1) % FOLD == iota((rows, LANES), 0) % FOLD,
        iota((rows, LANES), 1) < slots,
    )
    router = jnp.where(kept, router, 0.0).astype(BF16)
    lanes_left = out_ref.shape[-1] - pieces * width
    gather = iota((LANES, lanes_left), 0) // FOLD == iota((LANES, lanes_left), 1)
    parts.append(nn(router, gather.astype(F32).astype(BF16)))
    sent = jnp.concatenate(parts, axis=1)
    sent = sent.reshape(blocks, FOLD, sent.shape[1]).astype(BF16)
    for at, chip in enumerate(chip_order(blocks)):
        out_ref[(3 * blocks // 2 - 1 - chip) % blocks] = sent[at]


def merge_kernel(which_ref, mine_ref, other_ref, out_ref):
    which = which_ref[0]
    out_ref[:, 1 - which] = mine_ref[...]
    out_ref[:, which] = other_ref[...]


def finish_kernel(pieces, width, in_ref, pick_ref, grad_ref, router_ref):
    nodes = in_ref.shape[0]
    slot, hits = pair_maps(pick_ref[...], nodes)
    rows = in_ref[...].astype(F32).reshape(nodes * FOLD, in_ref.shape[2])
    base = pieces * width
    routed = jnp.zeros(slot.shape, F32)
    places = [placing(slot, piece) for piece in range(pieces)]
    for piece, place in enumerate(places):
        routed = routed + place * rows[:, base + piece : base + piece + 1]
    stacked = jnp.concatenate(
        [rows[:, piece * width : (piece + 1) * width] for piece in range(pieces)], axis=0
    )
    total = tn(stacked.astype(BF16), jnp.concatenate(places, axis=0).astype(BF16))
    grad_ref[...] = total.astype(BF16)
    router = [jnp.sum(jnp.where(hit, routed, 0.0), axis=0, keepdims=True) for hit in hits]
    router_ref[...] = jnp.concatenate(router, axis=0).astype(BF16)


def per_device(
    out_grad,
    node_pick,
    expert_pick,
    pick_weight,
    gate_weight,
    up_weight,
    down_weight,
    saved_gate,
    saved_up,
):
    nodes = lax.axis_size("node")
    local_count = lax.axis_size("local")
    tokens, width = out_grad.shape
    groups = node_pick.shape[1]
    experts, units = gate_weight.shape[1], gate_weight.shape[3]
    slots = saved_gate.shape[1]
    chips = local_count // 2
    pieces = slots // FOLD
    tiles = units // LANES
    half = nodes // 2
    held = round_up(slots, 8)
    packed = tiles * slots
    block = round_up(pieces * width + 2 * pieces, LANES)
    place = lax.axis_index("local").astype(jnp.int32)
    own = place.reshape(1)
    mine = own & 1
    same_core = [[2 * chip + c for chip in chip_order(chips)] for c in range(2)]
    backwards = [[(half - 1 - at) % nodes for at in range(nodes)]]
    swap = [(at, at ^ 1) for at in range(local_count)]

    pick = node_pick.T
    gate_saved = saved_gate.reshape(slots, units)
    up_saved = saved_up.reshape(slots, units)
    down = jnp.swapaxes(down_weight[0], 1, 2)
    hbm = pl.BlockSpec(memory_space=pltpu.HBM)
    vmem = pl.BlockSpec(memory_space=pltpu.VMEM)
    smem = pl.BlockSpec(memory_space=pltpu.SMEM)

    sent = call(
        functools.partial(prepare_kernel, pieces),
        jax.ShapeDtypeStruct((nodes, FOLD, block), BF16),
        limit=VMEM_MOST,
        in_specs=[hbm] * 4,
        out_specs=vmem,
        scratch_shapes=[
            pltpu.VMEM((groups, tokens), jnp.int32),
            pltpu.VMEM((groups, 1, tokens), jnp.int32),
            pltpu.VMEM((groups, tokens), BF16),
            pltpu.VMEM((width, tokens), BF16),
            pltpu.SemaphoreType.DMA((4,)),
        ],
    )(pick, jnp.transpose(expert_pick, (1, 2, 0)), pick_weight[:, :, 0].T, out_grad.T)
    others = [lax.ppermute(weight[0], "local", swap) for weight in (gate_weight, up_weight)]

    def keep(after, limit, *weights):
        return call(
            keep_kernel,
            tuple(jax.ShapeDtypeStruct(weight.shape, BF16) for weight in weights),
            limit=limit,
            in_specs=[hbm] + [vmem] * len(weights),
            out_specs=(vmem,) * len(weights),
        )(after, *weights)

    others = keep(sent, VMEM_MOST, *others)
    (sent_down,) = keep(others[0], VMEM_LIMIT, down)
    other_down = lax.ppermute(sent_down, "local", swap)
    arrived = lax.all_to_all(
        sent, "node", split_axis=0, concat_axis=0, axis_index_groups=backwards, tiled=True
    )
    arrived = arrived.reshape(half, 2, FOLD, block)

    def raw_part(rows, weight, dtype, *before):
        return call(
            functools.partial(raw_kernel, pieces, width, held),
            jax.ShapeDtypeStruct((half, packed, LANES), dtype),
            in_specs=[smem, vmem, vmem] + [vmem] * len(before),
            out_specs=vmem,
        )(mine, rows, weight, *before)

    received = lax.ppermute(arrived, "local", swap)
    partial = raw_part(arrived, down, F32)
    partial = raw_part(received, other_down, BF16, partial)
    parts = lax.all_to_all(
        partial, "local", split_axis=0, concat_axis=0, axis_index_groups=same_core, tiled=True
    )
    hidden = call(
        functools.partial(hidden_kernel, pieces, width),
        jax.ShapeDtypeStruct((chips, 2 * packed + 16, LANES), BF16),
        in_specs=[smem, vmem, vmem, vmem, vmem],
        out_specs=vmem,
    )(own, parts, arrived, gate_saved, up_saved)
    hidden_mine = lax.all_to_all(
        hidden, "local", split_axis=0, concat_axis=0, axis_index_groups=same_core, tiled=True
    )

    def back_part(gate, up):
        return call(
            functools.partial(back_kernel, pieces, width, held),
            jax.ShapeDtypeStruct((half, FOLD, block), BF16),
            in_specs=[vmem] * 3,
            out_specs=vmem,
        )(hidden_mine, gate, up)

    theirs = lax.ppermute(back_part(*others), "local", swap)
    back = call(
        merge_kernel,
        jax.ShapeDtypeStruct((half, 2, FOLD, block), BF16),
        in_specs=[smem, vmem, vmem],
        out_specs=vmem,
    )(mine, back_part(gate_weight[0], up_weight[0]), theirs)
    back = back.reshape(nodes, FOLD, block)
    returned = lax.all_to_all(
        back, "node", split_axis=0, concat_axis=0, axis_index_groups=backwards, tiled=True
    )
    grad, router = call(
        functools.partial(finish_kernel, pieces, width),
        (
            jax.ShapeDtypeStruct((width, tokens), BF16),
            jax.ShapeDtypeStruct((groups, tokens), BF16),
        ),
    )(returned, pick)
    return grad.T, router.T.reshape(tokens, groups, 1)


def solution(mesh):
    return jax.shard_map(
        per_device,
        mesh=mesh,
        in_specs=(
            P("node", "local"),
            P("node", None),
            P("node", None, None),
            P("node", None, None),
            P("node", None, "local", None),
            P("node", None, "local", None),
            P("node", None, None, "local"),
            P("node", "local", None, None),
            P("node", "local", None, None),
        ),
        out_specs=(P("node", "local"), P("node", None, None)),
        check_vma=False,
    )
```
